256 devices in a mesh: visit: 32 (over y, z), tile: 8 (over x, core).
Axes of the slice: x: 4, y: 4, z: 8, core: 2. Of those that a mesh axis runs over, the one named last changes fastest.
Arguments:
- science: float32 [32, 512, 4096], P('visit', 'tile'), may hold values from -8 to 8
- science_var: float32 [32, 512, 4096], P('visit', 'tile'), may hold values from 0.5 to 4
- template: float32 [32, 512, 4096], P('visit', 'tile'), may hold values from -8 to 8
- template_var: float32 [32, 512, 4096], P('visit', 'tile'), may hold values from 0.1 to 1
- intersection: int32 [32, 32, 1], replicated, may hold values from 0 to 31; in each aligned block of 32 rows (0 to 31, 32 to 63, ..., all dimensions but the last counted through in order) at most 2 rows name the same one
- col_offset: int32 [32, 32], replicated, may hold values from 0 to 3968
- basis_row: float32 [16, 41], replicated, may hold values from -1 to 1
- basis_col: float32 [16, 41], replicated, may hold values from -1 to 1
- coef_sets: float32 [8, 16], replicated, may hold values from -1.5 to 1.5
- tile_coef: int32 [32, 8], replicated, may hold values from 0 to 7
Outputs:
- difference: float32 [32, 512, 4096], P('visit', 'tile')
- difference_var: float32 [32, 512, 4096], P('visit', 'tile')
The draws below stay inside these ranges and needn't reach their ends.
Inputs may be any that keep to these rules, and one draw needn't show every extreme that they name: `intersection`: no visit takes more than 2 of its 32 pieces from one owner, and some visit takes exactly 2 from one owner.
All inputs are finite; a program needn't handle non-finite values.
Results may differ from the reference program's by a relative error of at most 0.0003.
Values sent between devices are 32-bit elements; how exact they have to be, the bound alone decides.
A program may use at most 320 MiB of HBM per device.

```python
import math
import jax
import jax.numpy as jnp
import numpy as np
from jax import lax

TR = 64
PIECE = 128
KP = 32
KW = 41
NB = 16
NSETS = 8
CAP = 2
VISITS = 32
TILES = 8
HEIGHT = 512
WIDTH = 4096
N_VISIT = 32


def with_ends(result, stream_key, least, top_value):
    place = [jax.random.randint(jax.random.fold_in(stream_key, axis), (), 0, length) for axis, length in enumerate(result.shape)]
    main_axis = result.shape.index(max(result.shape))
    beside = place[:main_axis] + [(place[main_axis] + 1) % result.shape[main_axis]] + place[main_axis + 1:]
    return result.at[tuple(place)].set(least).at[tuple(beside)].set(top_value)


def levels(key, extent, cuts, smallest, high):
    loudness = 1.0
    for position, blocks in cuts:
        draws = jax.random.uniform(jax.random.fold_in(jax.random.fold_in(key, 6), position), (blocks,), jnp.float32, smallest / len(cuts), high / len(cuts))
        loudness = loudness * jnp.repeat(jnp.exp(draws), extent[position] // blocks).reshape((-1,) + (1,) * (len(extent) - 1 - position))
    return loudness


def shared_out(stream_key, own, number, rows, count, top, reach, slope):
    ranking = jax.random.permutation(stream_key, count)
    packed, common = load_shares(count, rows * top, reach, slope, True), load_shares(count, rows * top, reach, slope, False)
    places = jnp.arange(count)

    def named(tallies, offset_by):
        used = int((tallies > 0).sum())
        fixed = max(1, used // 4)
        passed = fixed + (places - fixed + offset_by * (used - fixed)) % max(1, count - fixed)
        return jnp.zeros((count,), jnp.int32).at[ranking[jnp.where(places < fixed, places, passed)]].set(jnp.asarray(tallies, jnp.int32))

    tallies = jnp.where(number % 4 == 0, named(packed, number // 4), named(common, number - number // 4 - 1))
    mixed = jax.random.permutation(jax.random.fold_in(own, 3), count)
    giver, sink = mixed[0:count // 2 * 2:2], mixed[1:count // 2 * 2:2]
    slack = jnp.minimum(tallies[giver] - 1, reach - tallies[sink]) // 2
    slack = jnp.where((giver == ranking[0]) | (sink == ranking[0]) | (tallies[sink] == 0), 0, jnp.maximum(slack, 0))
    passed = jax.random.randint(jax.random.fold_in(own, 4), (count // 2,), 0, 1 << 20) % (slack + 1)
    tallies = tallies.at[giver].add(-passed).at[sink].add(passed)
    items = jnp.searchsorted(jnp.cumsum(tallies), jnp.arange(rows * top), side="right").astype(jnp.int32)
    listing = items.reshape(top, rows).T
    listing = listing[jax.random.permutation(jax.random.fold_in(own, 1), rows)]
    offset_by = jax.random.randint(jax.random.fold_in(own, 2), (rows, 1), 0, top)
    return jnp.take_along_axis(listing, (jnp.arange(top)[None, :] + offset_by) % top, axis=1)


def load_shares(count, total, reach, skew, full):
    portions = [(1 << 20) // math.isqrt(standing ** skew) + 1 for standing in range(1, count + 1)]
    largest = reach if full else min(reach, max(-(-total // count), total * portions[0] // sum(portions)))
    least = 1 if total - largest >= count - 1 else 0
    counts, spare = [largest] + [least] * (count - 1), total - largest - least * (count - 1)
    while spare > 0:
        movable = [i for i in range(1, count) if counts[i] < largest] or [i for i in range(1, count) if counts[i] < reach]
        whole, budget = sum([portions[i] for i in movable]), spare
        for i in movable:
            extra = min(reach - counts[i], max(1, budget * portions[i] // whole), spare)
            counts[i] = counts[i] + extra
            spare = spare - extra
    return np.array(counts)


def scatter_about(own_key, dims, deviation, bound, split=(), kind=jnp.bfloat16):
    entries = deviation * jax.random.normal(own_key, dims, jnp.float32)
    if split:
        entries = entries * levels(own_key, dims, split, -0.22, 0.18)
    return jnp.clip(entries, -bound, bound).astype(kind)


def setup_inputs(seed: int = 0) -> dict:
    key_of = jax.random.split(jax.random.key(seed), 11)
    science = scatter_about(key_of[0], (VISITS, HEIGHT, WIDTH), 1.0, 8.0, ((0, 32), (1, 8)), jnp.float32)
    science_var = jnp.clip(jnp.exp(math.log(4.0) - 2.0794415 * jax.random.uniform(key_of[1], (VISITS, HEIGHT, WIDTH), jnp.float32) ** levels(key_of[1], (VISITS, HEIGHT, WIDTH), ((0, 32), (1, 8)), -0.2, 0.2)), 0.5, 4.0)
    template = scatter_about(key_of[2], (VISITS, HEIGHT, WIDTH), 1.0, 8.0, ((0, 32), (1, 8)), jnp.float32)
    template_var = jnp.clip(jnp.exp(math.log(1.0) - 2.3025851 * jax.random.uniform(key_of[3], (VISITS, HEIGHT, WIDTH), jnp.float32) ** levels(key_of[3], (VISITS, HEIGHT, WIDTH), ((0, 32), (1, 8)), -0.2, 0.2)), 0.1, 1.0)
    intersection_keys = jax.random.split(jax.random.fold_in(key_of[4], 1), VISITS * KP // KP)
    intersection_turns = jax.random.permutation(jax.random.fold_in(key_of[4], 3), VISITS * KP // KP)
    intersection = jax.vmap(lambda own, number: shared_out(jax.random.fold_in(key_of[4], 2), own, number, KP, N_VISIT, 1, CAP, 2))(intersection_keys, intersection_turns).reshape((VISITS, KP, 1))
    col_offset = with_ends(jax.random.randint(key_of[5], (VISITS, KP), 0, KP * PIECE - PIECE + 1), jax.random.fold_in(key_of[5], 1), 0, KP * PIECE - PIECE).astype(jnp.int32)
    basis_row = scatter_about(key_of[6], (NB, KW), KW ** -0.5, 1.0, (), jnp.float32)
    basis_col = scatter_about(key_of[7], (NB, KW), KW ** -0.5, 1.0, (), jnp.float32)
    coef_sets = scatter_about(key_of[8], (NSETS, NB), NB ** -0.5, 1.5, (), jnp.float32)
    tile_coef = with_ends(jax.random.randint(key_of[9], (VISITS, TILES), 0, NSETS), jax.random.fold_in(key_of[9], 1), 0, NSETS - 1).astype(jnp.int32)
    return dict(science=science, science_var=science_var, template=template, template_var=template_var, intersection=intersection, col_offset=col_offset, basis_row=basis_row, basis_col=basis_col, coef_sets=coef_sets, tile_coef=tile_coef)


def reference(science, science_var, template, template_var, intersection, col_offset, basis_row, basis_col, coef_sets, tile_coef):
    margin = (KW - 1) // 2
    kernel_sets = jnp.einsum("sb,ba,bc->sac", coef_sets, basis_row, basis_col, precision=lax.Precision.HIGHEST)
    power_sets = jnp.sum(kernel_sets * kernel_sets, axis=(1, 2))
    zero_index = jnp.zeros((), jnp.int32)

    def one_visit(visit_index):
        owners = intersection[visit_index, :, 0].astype(jnp.int32)
        offsets = col_offset[visit_index].astype(jnp.int32)

        def cut_piece(owner, offset):
            fluxes = lax.dynamic_slice(template, (owner, zero_index, offset), (1, HEIGHT, PIECE))[0]
            spread = lax.dynamic_slice(template_var, (owner, zero_index, offset), (1, HEIGHT, PIECE))[0]
            return fluxes, spread

        pieces, pieces_var = jax.vmap(cut_piece)(owners, offsets)
        assembled = pieces.transpose(1, 0, 2).reshape(HEIGHT, WIDTH)
        assembled_var = pieces_var.transpose(1, 0, 2).reshape(HEIGHT, WIDTH)
        padded = jnp.pad(assembled, margin)

        def one_tile(tile_index):
            window = lax.dynamic_slice(padded, ((tile_index * TR).astype(jnp.int32), zero_index), (TR + 2 * margin, WIDTH + 2 * margin))
            chosen = tile_coef[visit_index, tile_index]
            kernel = kernel_sets[chosen]
            matched = lax.conv_general_dilated(window[None, None], kernel[None, None], (1, 1), "VALID", precision=lax.Precision.HIGHEST)[0, 0]
            return matched, power_sets[chosen]

        matched_all, powers = lax.map(one_tile, jnp.arange(TILES, dtype=jnp.int32))
        convolved = matched_all.reshape(HEIGHT, WIDTH)
        power_rows = jnp.repeat(powers, TR)
        difference = science[visit_index] - convolved
        difference_var = science_var[visit_index] + power_rows[:, None] * assembled_var
        return difference, difference_var

    difference, difference_var = lax.map(one_visit, jnp.arange(VISITS, dtype=jnp.int32))
    return difference, difference_var
```

```python
import functools

import jax
import jax.numpy as jnp
from jax import lax
from jax.experimental import pallas as pl
from jax.experimental.pallas import tpu as pltpu
from jax.sharding import PartitionSpec as P

MESH = pl.DeviceIdType.MESH
F32 = jnp.float32
BF16 = jnp.bfloat16

TR = 64
PIECE = 128
KP = 32
KW = 41
MARGIN = 20
NB = 16
NSETS = 8
TILES = 8
WIDTH = 4096
NY = 4
NZ = 8
CAP = 2
PER_ROW = NZ * CAP
CHUNK = 16
PARTS = TR // CHUNK
NC = 2 * PARTS
HALO = 24
XROWS = 128
WIN = 384
OUTW = 256
NWIN = WIDTH // OUTW
XBLOCKS = 34
GROUP = 4
NGROUPS = NB // GROUP


def pack_kernel(starts, flux, var, out):
    row = lax.rem(lax.axis_index("visit") // NZ + pl.program_id(0), NY)
    lane = lax.broadcasted_iota(jnp.int32, (TR, PIECE), 1)

    def one(slot, _):
        start = starts[row * PER_ROW + slot]
        block = start // PIECE
        shift = lax.rem(start, PIECE)
        low = pl.multiple_of(block * PIECE, PIECE)
        high = pl.multiple_of(jnp.minimum(block + 1, KP - 1) * PIECE, PIECE)
        turn = PIECE - shift
        for plane, ref in enumerate((flux, var)):
            piece = jnp.where(
                lane < turn,
                pltpu.roll(ref[:, pl.ds(low, PIECE)], turn, 1),
                pltpu.roll(ref[:, pl.ds(high, PIECE)], turn, 1),
            )
            for part in range(PARTS):
                out[plane * PARTS + part, 0, slot] = piece[part * CHUNK : (part + 1) * CHUNK]
        return 0

    lax.fori_loop(0, PER_ROW, one, 0)


def pack(starts, flux, var):
    return pl.pallas_call(
        pack_kernel,
        grid_spec=pltpu.PrefetchScalarGridSpec(
            num_scalar_prefetch=1,
            grid=(NY,),
            in_specs=[pl.BlockSpec((TR, WIDTH), lambda r, s: (0, 0))] * 2,
            out_specs=pl.BlockSpec((NC, 1, PER_ROW, CHUNK, PIECE), lambda r, s: (0, r, 0, 0, 0)),
        ),
        out_shape=jax.ShapeDtypeStruct((NC, NY, PER_ROW, CHUNK, PIECE), F32),
        compiler_params=pltpu.CompilerParams(vmem_limit_bytes=32 << 20),
        name="pack",
    )(starts, flux, var)


def split(x):
    high = x.astype(BF16)
    return high, (x - high.astype(F32)).astype(BF16)


def main_kernel(slots, *refs):
    (shift_of, place_of, pick_of, tile_coef, coefs, packed, brow, bcol) = refs[:8]
    conv, var_out, power = refs[8:11]
    yr, zs, zr = refs[11 : 11 + NC], refs[11 + NC : 11 + 2 * NC], refs[11 + 2 * NC : 11 + 3 * NC]
    (x_full, x_split, row_band, cb_high, cb_low, rw_high, rw_low, acc) = refs[11 + 3 * NC : 19 + 3 * NC]
    (own_sem, ys_sem, yr_sem, zs_sem, zr_sem, hs_sem, hr_sem) = refs[19 + 3 * NC :]

    me = lax.axis_index("visit")
    tile = lax.axis_index("tile")
    y, z = me // NZ, lax.rem(me, NZ)

    def y_peer(r):
        return (lax.rem(y + r, NY) * NZ + z, tile)

    def z_peer(d):
        return (y * NZ + lax.rem(z + d, NZ), tile)

    def t_peer(s):
        return (me, lax.rem(tile + s + TILES, TILES))

    barrier = pltpu.get_barrier_semaphore()
    peers = [y_peer(r) for r in range(1, NY)] + [z_peer(d) for d in range(1, NZ)] + [t_peer(1), t_peer(-1)]
    for peer in peers:
        pl.semaphore_signal(barrier, inc=1, device_id=peer, device_id_type=MESH)
    pl.semaphore_wait(barrier, len(peers))

    def y_copy(c, r):
        return pltpu.make_async_remote_copy(
            src_ref=packed.at[c, r],
            dst_ref=yr[c].at[pl.ds(r * PER_ROW, PER_ROW)],
            send_sem=ys_sem.at[c, r - 1],
            recv_sem=yr_sem.at[c, r - 1],
            device_id=y_peer(r),
            device_id_type=MESH,
        )

    def own_copy(c):
        return pltpu.make_async_copy(packed.at[c, 0], yr[c].at[pl.ds(0, PER_ROW)], own_sem.at[c])

    def z_copy(c, d):
        return pltpu.make_async_remote_copy(
            src_ref=zs[c].at[pl.ds(d * slots, slots)],
            dst_ref=zr[c].at[pl.ds(d * slots, slots)],
            send_sem=zs_sem.at[c, d - 1],
            recv_sem=zr_sem.at[c, d - 1],
            device_id=z_peer(d),
            device_id_type=MESH,
        )

    def halo_copy(which):
        source, target, step = ((TR, 0, 1), (HALO, HALO + TR, -1))[which]
        return pltpu.make_async_remote_copy(
            src_ref=x_full.at[pl.ds(source, HALO)],
            dst_ref=x_full.at[pl.ds(target, HALO)],
            send_sem=hs_sem.at[which],
            recv_sem=hr_sem.at[which],
            device_id=t_peer(step),
            device_id_type=MESH,
        )

    def y_start(c):
        for r in (2, 1, 3):
            y_copy(c, r).start()
        own_copy(c).start()

    def forward(c):
        own_copy(c).wait()
        for r in range(1, NY):
            y_copy(c, r).wait_recv()

        def one(e, _):
            half = (e + 1) // 2
            d = NZ // 2 + jnp.where(lax.rem(e, 2) == 1, -half, half)
            base = (y * NZ + lax.rem(z + d, NZ)) * NZ
            for p in range(slots):
                zs[c][d * slots + p] = yr[c][pick_of[base + p]]
            z_copy(c, d).start()
            return 0

        lax.fori_loop(0, NZ - 1, one, 0)
        for p in range(slots):
            zr[c][p] = yr[c][pick_of[me * NZ + p]]

    def assemble(c, out, row):
        for d in range(1, NZ):
            z_copy(c, d).wait_recv()

        def one(k, _):
            at = shift_of[me * KP + k] * slots + place_of[me * KP + k]
            out[pl.ds(row, CHUNK), pl.ds(pl.multiple_of(k * PIECE, PIECE), PIECE)] = zr[c][at]
            return 0

        lax.fori_loop(0, KP, one, 0)

    chosen = tile_coef[me * TILES + tile]

    def bands():
        rows = [coefs[chosen * NB + b] * brow[b : b + 1, :] for b in range(NB)]
        for b in range(NB):
            band = pltpu.roll(jnp.broadcast_to(rows[b], (TR, PIECE)), 0, 1, stride=1, stride_axis=0)
            high, low = split(band)
            row_band[b * TR : (b + 1) * TR, 0:PIECE] = high
            row_band[b * TR : (b + 1) * TR, PIECE : 2 * PIECE] = low
            row_band[b * TR : (b + 1) * TR, 2 * PIECE : 3 * PIECE] = high
        whole = lax.dot_general(
            jnp.concatenate(rows, axis=0),
            bcol[...],
            (((0,), (0,)), ((), ())),
            precision=lax.Precision.HIGHEST,
            preferred_element_type=F32,
        )
        power[...] = jnp.full((8, PIECE), jnp.sum(whole * whole), F32)

        def one(b, _):
            line = bcol[pl.ds(b, 1), :]
            for part in range(WIN // 128):
                turned = pltpu.roll(
                    jnp.broadcast_to(line, (128, OUTW)), (part * 128) % OUTW, 1, stride=1, stride_axis=0
                )
                tap = (
                    lax.broadcasted_iota(jnp.int32, (128, OUTW), 0)
                    + part * 128
                    - lax.broadcasted_iota(jnp.int32, (128, OUTW), 1)
                )
                high, low = split(jnp.where((tap >= 0) & (tap < KW), turned, 0.0))
                place = pl.ds(pl.multiple_of(b * WIN + part * 128, 128), 128)
                cb_high[place, :] = high
                cb_low[place, :] = low
            return 0

        lax.fori_loop(0, NB, one, 0)

    def expand():
        row = lax.broadcasted_iota(jnp.int32, (XROWS, PIECE), 0)
        lane = lax.broadcasted_iota(jnp.int32, (XROWS, PIECE), 1)
        first = jnp.where(tile == 0, HALO, 0)
        last = jnp.where(tile == TILES - 1, HALO + TR, HALO + TR + HALO)
        rows_in = (row >= first) & (row < last)

        def one(j, _):
            here = pl.multiple_of(jnp.minimum(j, KP - 1) * PIECE, PIECE)
            before = pl.multiple_of(jnp.minimum(jnp.maximum(j - 1, 0), KP - 1) * PIECE, PIECE)
            both = jnp.where(
                lane < MARGIN,
                pltpu.roll(x_full[:, pl.ds(before, PIECE)], MARGIN, 1),
                pltpu.roll(x_full[:, pl.ds(here, PIECE)], MARGIN, 1),
            )
            column = j * PIECE + lane - MARGIN
            high, low = split(jnp.where(rows_in & (column >= 0) & (column < WIDTH), both, 0.0))
            place = pl.ds(pl.multiple_of(j * PIECE, PIECE), PIECE)
            x_split[0:XROWS, place] = high
            x_split[XROWS : 2 * XROWS, place] = high
            x_split[2 * XROWS : 3 * XROWS, place] = low
            return 0

        lax.fori_loop(0, XBLOCKS, one, 0)

    def convolve(g):
        def rows(m, _):
            high, low = split(
                jnp.dot(
                    row_band[g * GROUP * TR : (g + 1) * GROUP * TR, :],
                    x_split[:, pl.ds(pl.multiple_of(m * OUTW, OUTW), OUTW)],
                    preferred_element_type=F32,
                )
            )
            now = pl.ds(pl.multiple_of((m + 1) * TR, TR), TR)
            earlier = pl.ds(pl.multiple_of(m * TR, TR), TR)
            for out, value in ((rw_high, high), (rw_low, low)):
                for b in range(GROUP):
                    part = value[b * TR : (b + 1) * TR]
                    out[now, b * WIN : b * WIN + OUTW] = part
                    out[earlier, b * WIN + OUTW : (b + 1) * WIN] = part[:, 0 : WIN - OUTW]
            return 0

        lax.fori_loop(0, NWIN + 1, rows, 0)
        band = slice(g * GROUP * WIN, (g + 1) * GROUP * WIN)

        def cols(m, _):
            at = pl.ds(pl.multiple_of(TR + m * 512, TR), 512)
            high = rw_high[at, :]
            total = jnp.dot(high, cb_high[band, :], preferred_element_type=F32)
            total += jnp.dot(high, cb_low[band, :], preferred_element_type=F32)
            total += jnp.dot(rw_low[at, :], cb_high[band, :], preferred_element_type=F32)
            place = pl.ds(pl.multiple_of(m * 512, 512), 512)
            acc[place, :] = total if g == 0 else acc[place, :] + total
            return 0

        lax.fori_loop(0, NWIN * TR // 512, cols, 0)

    y_start(0)
    y_start(1)
    y_start(2)
    for c in range(NC):
        forward(c)
        if c + 3 < NC:
            y_start(c + 3)
        if c == PARTS - 1:
            bands()
        if c == NC - 3:
            for part in range(PARTS):
                assemble(part, x_full, HALO + part * CHUNK)
            halo_copy(0).start()
            halo_copy(1).start()
        if c == NC - 2:
            halo_copy(0).wait_recv()
            halo_copy(1).wait_recv()
            expand()
            convolve(0)
    for g in range(1, NGROUPS):
        convolve(g)
    for n in range(NWIN):
        conv[:, n * OUTW : (n + 1) * OUTW] = acc[n * TR : (n + 1) * TR, :]
    for part in range(PARTS):
        assemble(PARTS + part, var_out, part * CHUNK)
    halo_copy(0).wait_send()
    halo_copy(1).wait_send()
    for c in range(NC):
        for r in range(1, NY):
            y_copy(c, r).wait_send()
        for d in range(1, NZ):
            z_copy(c, d).wait_send()


def exchange(slots, shift_of, place_of, pick_of, tile_coef, coefs, packed, brow, bcol):
    smem = pl.BlockSpec(memory_space=pltpu.SMEM)
    vmem = pl.BlockSpec(memory_space=pltpu.VMEM)
    scratch = [pltpu.VMEM((NY * PER_ROW, CHUNK, PIECE), F32)] * NC
    scratch += [pltpu.VMEM((NZ * slots, CHUNK, PIECE), F32)] * (2 * NC)
    scratch += [
        pltpu.VMEM((XROWS, WIDTH), F32),
        pltpu.VMEM((3 * XROWS, XBLOCKS * PIECE), BF16),
        pltpu.VMEM((NB * TR, 3 * PIECE), BF16),
        pltpu.VMEM((NB * WIN, OUTW), BF16),
        pltpu.VMEM((NB * WIN, OUTW), BF16),
        pltpu.VMEM(((NWIN + 2) * TR, GROUP * WIN), BF16),
        pltpu.VMEM(((NWIN + 2) * TR, GROUP * WIN), BF16),
        pltpu.VMEM((NWIN * TR, OUTW), F32),
        pltpu.SemaphoreType.DMA((NC,)),
        pltpu.SemaphoreType.DMA((NC, NY - 1)),
        pltpu.SemaphoreType.DMA((NC, NY - 1)),
        pltpu.SemaphoreType.DMA((NC, NZ - 1)),
        pltpu.SemaphoreType.DMA((NC, NZ - 1)),
        pltpu.SemaphoreType.DMA((2,)),
        pltpu.SemaphoreType.DMA((2,)),
    ]
    return pl.pallas_call(
        functools.partial(main_kernel, slots),
        out_shape=(
            jax.ShapeDtypeStruct((TR, WIDTH), F32),
            jax.ShapeDtypeStruct((TR, WIDTH), F32),
            jax.ShapeDtypeStruct((8, PIECE), F32),
        ),
        in_specs=[smem] * 5 + [pl.BlockSpec(memory_space=pl.ANY)] + [vmem] * 2,
        out_specs=(vmem, vmem, vmem),
        scratch_shapes=scratch,
        compiler_params=pltpu.CompilerParams(
            collective_id=slots, has_side_effects=True, vmem_limit_bytes=56 << 20
        ),
        cost_estimate=pl.CostEstimate(flops=10**10, bytes_accessed=6 << 20, transcendentals=0),
        name=f"exchange_{slots}",
    )(shift_of, place_of, pick_of, tile_coef, coefs, packed, brow, bcol)


VARIANTS = (5, 6, 8)


def local(
    science,
    science_var,
    template,
    template_var,
    intersection,
    col_offset,
    basis_row,
    basis_col,
    coef_sets,
    tile_coef,
):
    me = lax.axis_index("visit")
    my_y, my_z = me // NZ, me % NZ
    owner = intersection[:, :, 0]
    column = owner % NZ
    earlier = jnp.arange(KP)[None, None, :] < jnp.arange(KP)[None, :, None]
    rank = jnp.sum(((owner[:, :, None] == owner[:, None, :]) & earlier).astype(jnp.int32), axis=2)
    place = jnp.sum(((column[:, :, None] == column[:, None, :]) & earlier).astype(jnp.int32), axis=2)
    mine = (owner == me)[:, None, :] & (rank[:, None, :] == jnp.arange(CAP)[None, :, None])
    starts = jnp.sum(jnp.where(mine, col_offset[:, None, :], 0), axis=2).reshape(-1)
    came_from = (my_y - owner // NZ) % NY
    visit_z = jnp.arange(KP, dtype=jnp.int32)[:, None] % NZ
    slot = came_from * PER_ROW + visit_z * CAP + rank
    here = (column == my_z)[:, None, :] & (place[:, None, :] == jnp.arange(NZ)[None, :, None])
    pick = jnp.sum(jnp.where(here, slot[:, None, :], 0), axis=2).reshape(-1)
    shift = ((visit_z - column) % NZ).reshape(-1)
    most = jnp.max(place) + 1

    packed = pack(starts, template[0], template_var[0])
    brow = jnp.pad(basis_row, ((0, 0), (HALO - MARGIN, PIECE - KW - HALO + MARGIN)))
    bcol = jnp.concatenate(
        [basis_col[:, 0:1], jnp.zeros((NB, OUTW - KW), F32), basis_col[:, :0:-1]], axis=1
    )
    which = sum((most > n).astype(jnp.int32) for n in VARIANTS[:-1])
    convolved, variance, power = lax.switch(
        which,
        [functools.partial(exchange, n) for n in VARIANTS],
        shift,
        place.reshape(-1),
        pick,
        tile_coef.reshape(-1),
        coef_sets.reshape(-1),
        packed,
        brow,
        bcol,
    )
    difference = science - convolved[None]
    difference_var = science_var + power[0, 0] * variance[None]
    return difference, difference_var


def solution(mesh):
    split3 = P("visit", "tile", None)
    return jax.shard_map(
        local,
        mesh=mesh,
        in_specs=(split3, split3, split3, split3, P(), P(), P(), P(), P(), P()),
        out_specs=(split3, split3),
        check_vma=False,
    )
```

```python
import functools

import jax
import jax.numpy as jnp
from jax import lax
from jax.experimental import pallas as pl
from jax.experimental.pallas import tpu as pltpu
from jax.sharding import PartitionSpec as P

MESH = pl.DeviceIdType.MESH
F32 = jnp.float32
BF16 = jnp.bfloat16

TR = 64
PIECE = 128
KP = 32
KW = 41
MARGIN = 20
NB = 16
NSETS = 8
TILES = 8
WIDTH = 4096
NY = 4
NZ = 8
CAP = 2
PER_ROW = NZ * CAP
CHUNK = 16
PARTS = TR // CHUNK
NC = 2 * PARTS
HALO = 24
XROWS = 128
WIN = 384
OUTW = 256
NWIN = WIDTH // OUTW
XBLOCKS = 34
HALVES = 2
HWIN = NWIN // HALVES


PLACE, STARTS, PICK, WHICH = KP, 2 * KP, 3 * KP, 4 * KP
VARIANTS = (5, 6, 8)


def plan_kernel(inter, offset, basis_row, basis_col, table, brow, bcol):
    me = lax.axis_index("visit")
    my_y, my_z = me // NZ, lax.rem(me, NZ)
    owner = inter[...]
    column = lax.rem(owner, NZ)
    lane = lax.broadcasted_iota(jnp.int32, (KP, KP), 1)
    visit_z = lax.rem(lax.broadcasted_iota(jnp.int32, (KP, KP), 0), NZ)
    rank = jnp.zeros((KP, KP), jnp.int32)
    place = jnp.zeros((KP, KP), jnp.int32)
    for k in range(KP - 1):
        later = lane > k
        rank += ((owner == owner[:, k : k + 1]) & later).astype(jnp.int32)
        place += ((column == column[:, k : k + 1]) & later).astype(jnp.int32)
    slot = lax.rem(my_y + NY - owner // NZ, NY) * PER_ROW + visit_z * CAP + rank
    starts = jnp.zeros((KP, KP), jnp.int32)
    for j in range(CAP):
        found = jnp.sum(jnp.where((owner == me) & (rank == j), offset[...], 0), axis=1, keepdims=True)
        starts = jnp.where(lane == j, found, starts)
    pick = jnp.zeros((KP, KP), jnp.int32)
    for p in range(NZ):
        found = jnp.sum(jnp.where((column == my_z) & (place == p), slot, 0), axis=1, keepdims=True)
        pick = jnp.where(lane == p, found, pick)
    most = jnp.max(place) + 1
    which = jnp.zeros((8, KP), jnp.int32)
    for n in VARIANTS[:-1]:
        which += (most > n).astype(jnp.int32)
    table[0:PLACE] = lax.rem(visit_z - column + NZ, NZ)
    table[PLACE:STARTS] = place
    table[STARTS:PICK] = starts
    table[PICK:WHICH] = pick
    table[WHICH:] = which

    def spread(values, width, at):
        tap = lax.broadcasted_iota(jnp.int32, (KW, width), 0)
        hot = lax.broadcasted_iota(jnp.int32, (KW, width), 1) == at(tap)
        return jnp.dot(
            values, hot.astype(F32), precision=lax.Precision.HIGHEST, preferred_element_type=F32
        )

    brow[...] = spread(basis_row[...], PIECE, lambda tap: tap + HALO - MARGIN)
    bcol[...] = spread(basis_col[...], OUTW, lambda tap: lax.rem(OUTW - tap, OUTW))


def plan(inter, offset, basis_row, basis_col):
    return pl.pallas_call(
        plan_kernel,
        out_shape=(
            jax.ShapeDtypeStruct((WHICH + 8, KP), jnp.int32),
            jax.ShapeDtypeStruct((NB, PIECE), F32),
            jax.ShapeDtypeStruct((NB, OUTW), F32),
        ),
        in_specs=[pl.BlockSpec(memory_space=pltpu.VMEM)] * 4,
        out_specs=(pl.BlockSpec(memory_space=pltpu.VMEM),) * 3,
        name="plan",
    )(inter, offset, basis_row, basis_col)


def split(x):
    high = x.astype(BF16)
    return high, (x - high.astype(F32)).astype(BF16)


def main_kernel(slots, *refs):
    table, tile_coef, coefs, flux_in, var_in, brow, bcol, conv, var_out = refs[:9]
    ys, yr, zs, zr = (refs[9 + n * NC : 9 + (n + 1) * NC] for n in range(4))
    strips, blocks = refs[9 + 4 * NC : 11 + 4 * NC], refs[11 + 4 * NC : 13 + 4 * NC]
    x_full, x_split, row_band, cb_high, cb_low, rw_high, rw_low = refs[13 + 4 * NC : 20 + 4 * NC]
    in_sem, ys_sem, yr_sem, zs_sem, zr_sem, hs_sem, hr_sem = refs[20 + 4 * NC :]

    me = lax.axis_index("visit")
    tile = lax.axis_index("tile")
    y, z = me // NZ, lax.rem(me, NZ)

    def y_peer(r):
        return (lax.rem(y + r, NY) * NZ + z, tile)

    def z_peer(d):
        return (y * NZ + lax.rem(z + d, NZ), tile)

    def t_peer(s):
        return (me, lax.rem(tile + s + TILES, TILES))

    inputs = [
        pltpu.make_async_copy(source, target, in_sem.at[n])
        for n, (source, target) in enumerate(zip((flux_in, var_in), strips))
    ]
    for copy in inputs:
        copy.start()
    barrier = pltpu.get_barrier_semaphore()
    peers = [y_peer(r) for r in range(1, NY)] + [z_peer(d) for d in range(1, NZ)] + [t_peer(1), t_peer(-1)]
    for peer in peers:
        pl.semaphore_signal(barrier, inc=1, device_id=peer, device_id_type=MESH)
    pl.semaphore_wait(barrier, len(peers))

    def y_copy(c, r):
        return pltpu.make_async_remote_copy(
            src_ref=ys[c].at[pl.ds((r - 1) * PER_ROW, PER_ROW)],
            dst_ref=yr[c].at[pl.ds(r * PER_ROW, PER_ROW)],
            send_sem=ys_sem.at[c, r - 1],
            recv_sem=yr_sem.at[c, r - 1],
            device_id=y_peer(r),
            device_id_type=MESH,
        )

    def z_copy(c, d):
        return pltpu.make_async_remote_copy(
            src_ref=zs[c].at[pl.ds(d * slots, slots)],
            dst_ref=zr[c].at[pl.ds(d * slots, slots)],
            send_sem=zs_sem.at[c, d - 1],
            recv_sem=zr_sem.at[c, d - 1],
            device_id=z_peer(d),
            device_id_type=MESH,
        )

    def halo_copy(which):
        source, target, step = ((TR, 0, 1), (HALO, HALO + TR, -1))[which]
        return pltpu.make_async_remote_copy(
            src_ref=x_full.at[pl.ds(source, HALO)],
            dst_ref=x_full.at[pl.ds(target, HALO)],
            send_sem=hs_sem.at[which],
            recv_sem=hr_sem.at[which],
            device_id=t_peer(step),
            device_id_type=MESH,
        )

    lane = lax.broadcasted_iota(jnp.int32, (CHUNK, PIECE), 1)

    def take_in(plane):
        inputs[plane].wait()

        def one(k, _):
            at = pl.ds(pl.multiple_of(k * PIECE, PIECE), PIECE)
            blocks[plane][k] = strips[plane][:, at]
            return 0

        lax.fori_loop(0, KP, one, 0)

    def cut(c, r, out, first):
        source = blocks[c // PARTS]
        rows = slice(c % PARTS * CHUNK, (c % PARTS + 1) * CHUNK)
        visits = STARTS + lax.rem(y + r, NY) * NZ

        def one(vz, _):
            for j in range(CAP):
                start = table[visits + vz, j]
                block = start // PIECE
                shift = jnp.full((CHUNK, PIECE), start - block * PIECE, jnp.int32)
                piece = jnp.where(
                    lane >= shift, source[block, rows, :], source[jnp.minimum(block + 1, KP - 1), rows, :]
                )
                for bit in range(7):
                    turned = pltpu.roll(piece, PIECE - (1 << bit), 1)
                    piece = jnp.where((shift & (1 << bit)) != 0, turned, piece)
                out[first + vz * CAP + j] = piece
            return 0

        lax.fori_loop(0, NZ, one, 0)

    def y_start(c):
        def one(r, _):
            cut(c, r, ys[c], (r - 1) * PER_ROW)
            y_copy(c, r).start()
            return 0

        lax.fori_loop(1, NY, one, 0)
        cut(c, 0, yr[c], 0)

    def forward(c):
        for r in range(1, NY):
            y_copy(c, r).wait_recv()

        def one(e, _):
            half = (e + 1) // 2
            d = NZ // 2 + jnp.where(lax.rem(e, 2) == 1, -half, half)
            row = PICK + y * NZ + lax.rem(z + d, NZ)
            for p in range(slots):
                zs[c][d * slots + p] = yr[c][table[row, p]]
            z_copy(c, d).start()
            return 0

        lax.fori_loop(0, NZ - 1, one, 0)
        for p in range(slots):
            zr[c][p] = yr[c][table[PICK + me, p]]

    def assemble(c, out, row, scale=None):
        for d in range(1, NZ):
            z_copy(c, d).wait_recv()

        def one(k, _):
            piece = zr[c][table[me, k] * slots + table[PLACE + me, k]]
            at = pl.ds(pl.multiple_of(k * PIECE, PIECE), PIECE)
            out[pl.ds(row, CHUNK), at] = piece if scale is None else piece * scale
            return 0

        lax.fori_loop(0, KP, one, 0)

    chosen = tile_coef[me, tile]

    def bands():
        rows = [coefs[chosen, b] * brow[b : b + 1, :] for b in range(NB)]
        for b in range(NB):
            band = pltpu.roll(jnp.broadcast_to(rows[b], (TR, PIECE)), 0, 1, stride=1, stride_axis=0)
            high, low = split(band)
            row_band[b * TR : (b + 1) * TR, 0:PIECE] = high
            row_band[b * TR : (b + 1) * TR, PIECE : 2 * PIECE] = low
            row_band[b * TR : (b + 1) * TR, 2 * PIECE : 3 * PIECE] = high
        whole = lax.dot_general(
            jnp.concatenate(rows, axis=0),
            bcol[...],
            (((0,), (0,)), ((), ())),
            precision=lax.Precision.HIGHEST,
            preferred_element_type=F32,
        )
        def one(b, _):
            line = bcol[pl.ds(b, 1), :]
            for part in range(WIN // 128):
                turned = pltpu.roll(
                    jnp.broadcast_to(line, (128, OUTW)), (part * 128) % OUTW, 1, stride=1, stride_axis=0
                )
                tap = (
                    lax.broadcasted_iota(jnp.int32, (128, OUTW), 0)
                    + part * 128
                    - lax.broadcasted_iota(jnp.int32, (128, OUTW), 1)
                )
                high, low = split(jnp.where((tap >= 0) & (tap < KW), turned, 0.0))
                place = pl.ds(pl.multiple_of(b * WIN + part * 128, 128), 128)
                cb_high[place, :] = high
                cb_low[place, :] = low
            return 0

        lax.fori_loop(0, NB, one, 0)
        return jnp.sum(whole * whole)

    def expand():
        row = lax.broadcasted_iota(jnp.int32, (XROWS, PIECE), 0)
        lane = lax.broadcasted_iota(jnp.int32, (XROWS, PIECE), 1)
        first = jnp.where(tile == 0, HALO, 0)
        last = jnp.where(tile == TILES - 1, HALO + TR, HALO + TR + HALO)
        rows_in = (row >= first) & (row < last)

        def one(j, _):
            here = pl.multiple_of(jnp.minimum(j, KP - 1) * PIECE, PIECE)
            before = pl.multiple_of(jnp.minimum(jnp.maximum(j - 1, 0), KP - 1) * PIECE, PIECE)
            both = jnp.where(
                lane < MARGIN,
                pltpu.roll(x_full[:, pl.ds(before, PIECE)], MARGIN, 1),
                pltpu.roll(x_full[:, pl.ds(here, PIECE)], MARGIN, 1),
            )
            column = j * PIECE + lane - MARGIN
            high, low = split(jnp.where(rows_in & (column >= 0) & (column < WIDTH), both, 0.0))
            place = pl.ds(pl.multiple_of(j * PIECE, PIECE), PIECE)
            x_split[0:XROWS, place] = high
            x_split[XROWS : 2 * XROWS, place] = high
            x_split[2 * XROWS : 3 * XROWS, place] = low
            return 0

        lax.fori_loop(0, XBLOCKS, one, 0)

    def convolve(h):
        def rows(m, _):
            high, low = split(
                jnp.dot(
                    row_band[...],
                    x_split[:, pl.ds(pl.multiple_of((h * HWIN + m) * OUTW, OUTW), OUTW)],
                    preferred_element_type=F32,
                )
            )
            now = pl.ds(pl.multiple_of((m + 1) * TR, TR), TR)
            before = pl.ds(pl.multiple_of(m * TR, TR), TR)
            for out, value in ((rw_high, high), (rw_low, low)):
                for b in range(NB):
                    part = value[b * TR : (b + 1) * TR]
                    out[now, b * WIN : b * WIN + OUTW] = part
                    out[before, b * WIN + OUTW : (b + 1) * WIN] = part[:, 0 : WIN - OUTW]
            return 0

        lax.fori_loop(0, HWIN + 1, rows, 0)
        at = slice(TR, TR + HWIN * TR)
        total = jnp.dot(rw_high[at, :], cb_high[...], preferred_element_type=F32)
        total += jnp.dot(rw_high[at, :], cb_low[...], preferred_element_type=F32)
        total += jnp.dot(rw_low[at, :], cb_high[...], preferred_element_type=F32)
        for n in range(HWIN):
            first = (h * HWIN + n) * OUTW
            conv[:, first : first + OUTW] = total[n * TR : (n + 1) * TR, :]

    take_in(0)
    y_start(0)
    y_start(1)
    y_start(2)
    for c in range(NC):
        forward(c)
        if c + 3 == PARTS:
            take_in(1)
        if c + 3 < NC:
            y_start(c + 3)
        if c == PARTS - 1:
            power = bands()
        if c == NC - 3:
            for part in range(PARTS):
                assemble(part, x_full, HALO + part * CHUNK)
            halo_copy(0).start()
            halo_copy(1).start()
        if c == NC - 2:
            halo_copy(0).wait_recv()
            halo_copy(1).wait_recv()
            expand()
            convolve(0)
    convolve(1)
    for part in range(PARTS):
        assemble(PARTS + part, var_out, part * CHUNK, power)
    halo_copy(0).wait_send()
    halo_copy(1).wait_send()
    for c in range(NC):
        for r in range(1, NY):
            y_copy(c, r).wait_send()
        for d in range(1, NZ):
            z_copy(c, d).wait_send()


def exchange(slots, table, tile_coef, coefs, flux, var, brow, bcol):
    smem = pl.BlockSpec(memory_space=pltpu.SMEM)
    vmem = pl.BlockSpec(memory_space=pltpu.VMEM)
    hbm = pl.BlockSpec(memory_space=pl.ANY)
    scratch = [pltpu.VMEM(((NY - 1) * PER_ROW, CHUNK, PIECE), F32)] * NC
    scratch += [pltpu.VMEM((NY * PER_ROW, CHUNK, PIECE), F32)] * NC
    scratch += [pltpu.VMEM((NZ * slots, CHUNK, PIECE), F32)] * (2 * NC)
    scratch += [
        pltpu.VMEM((TR, WIDTH), F32),
        pltpu.VMEM((TR, WIDTH), F32),
        pltpu.VMEM((KP, TR, PIECE), F32),
        pltpu.VMEM((KP, TR, PIECE), F32),
        pltpu.VMEM((XROWS, WIDTH), F32),
        pltpu.VMEM((3 * XROWS, XBLOCKS * PIECE), BF16),
        pltpu.VMEM((NB * TR, 3 * PIECE), BF16),
        pltpu.VMEM((NB * WIN, OUTW), BF16),
        pltpu.VMEM((NB * WIN, OUTW), BF16),
        pltpu.VMEM(((HWIN + 2) * TR, NB * WIN), BF16),
        pltpu.VMEM(((HWIN + 2) * TR, NB * WIN), BF16),
        pltpu.SemaphoreType.DMA((2,)),
        pltpu.SemaphoreType.DMA((NC, NY - 1)),
        pltpu.SemaphoreType.DMA((NC, NY - 1)),
        pltpu.SemaphoreType.DMA((NC, NZ - 1)),
        pltpu.SemaphoreType.DMA((NC, NZ - 1)),
        pltpu.SemaphoreType.DMA((2,)),
        pltpu.SemaphoreType.DMA((2,)),
    ]
    return pl.pallas_call(
        functools.partial(main_kernel, slots),
        out_shape=(
            jax.ShapeDtypeStruct((TR, WIDTH), F32),
            jax.ShapeDtypeStruct((TR, WIDTH), F32),
        ),
        in_specs=[smem] * 3 + [hbm] * 2 + [vmem] * 2,
        out_specs=(vmem, vmem),
        scratch_shapes=scratch,
        compiler_params=pltpu.CompilerParams(
            collective_id=slots, has_side_effects=True, vmem_limit_bytes=60 << 20
        ),
        cost_estimate=pl.CostEstimate(flops=10**10, bytes_accessed=6 << 20, transcendentals=0),
        name=f"exchange_{slots}",
    )(table, tile_coef, coefs, flux, var, brow, bcol)


def local(
    science,
    science_var,
    template,
    template_var,
    intersection,
    col_offset,
    basis_row,
    basis_col,
    coef_sets,
    tile_coef,
):
    table, brow, bcol = plan(intersection[:, :, 0], col_offset, basis_row, basis_col)
    convolved, variance = lax.switch(
        table[WHICH, 0],
        [functools.partial(exchange, n) for n in VARIANTS],
        table,
        tile_coef,
        coef_sets,
        template[0],
        template_var[0],
        brow,
        bcol,
    )
    return science - convolved[None], science_var + variance[None]


def solution(mesh):
    split3 = P("visit", "tile", None)
    return jax.shard_map(
        local,
        mesh=mesh,
        in_specs=(split3, split3, split3, split3, P(), P(), P(), P(), P(), P()),
        out_specs=(split3, split3),
        check_vma=False,
    )
```

```python
import functools

import jax
import jax.numpy as jnp
from jax import lax
from jax.experimental import pallas as pl
from jax.experimental.pallas import tpu as pltpu
from jax.sharding import PartitionSpec as P

MESH = pl.DeviceIdType.MESH
F32 = jnp.float32
BF16 = jnp.bfloat16

TR = 64
PIECE = 128
KP = 32
KW = 41
MARGIN = 20
NB = 16
NSETS = 8
TILES = 8
WIDTH = 4096
NY = 4
NZ = 8
CAP = 2
PER_ROW = NZ * CAP
CHUNK = 16
PARTS = TR // CHUNK
NC = 2 * PARTS
HALO = 24
XROWS = 128
WIN = 384
OUTW = 256
NWIN = WIDTH // OUTW
XBLOCKS = 34
HALVES = 2
HWIN = NWIN // HALVES


PLACE, STARTS, PICK, WHICH = KP, 2 * KP, 3 * KP, 4 * KP
VARIANTS = (5, 6, 8)


def plan_kernel(inter, offset, basis_row, basis_col, table, brow, bcol):
    me = lax.axis_index("visit")
    my_y, my_z = me // NZ, lax.rem(me, NZ)
    owner = inter[...]
    column = lax.rem(owner, NZ)
    lane = lax.broadcasted_iota(jnp.int32, (KP, KP), 1)
    visit_z = lax.rem(lax.broadcasted_iota(jnp.int32, (KP, KP), 0), NZ)
    rank = jnp.zeros((KP, KP), jnp.int32)
    place = jnp.zeros((KP, KP), jnp.int32)
    for k in range(KP - 1):
        later = lane > k
        rank += ((owner == owner[:, k : k + 1]) & later).astype(jnp.int32)
        place += ((column == column[:, k : k + 1]) & later).astype(jnp.int32)
    slot = lax.rem(my_y + NY - owner // NZ, NY) * PER_ROW + visit_z * CAP + rank
    starts = jnp.zeros((KP, KP), jnp.int32)
    for j in range(CAP):
        found = jnp.sum(jnp.where((owner == me) & (rank == j), offset[...], 0), axis=1, keepdims=True)
        starts = jnp.where(lane == j, found, starts)
    pick = jnp.zeros((KP, KP), jnp.int32)
    for p in range(NZ):
        found = jnp.sum(jnp.where((column == my_z) & (place == p), slot, 0), axis=1, keepdims=True)
        pick = jnp.where(lane == p, found, pick)
    most = jnp.max(place) + 1
    which = jnp.zeros((8, KP), jnp.int32)
    for n in VARIANTS[:-1]:
        which += (most > n).astype(jnp.int32)
    table[0:PLACE] = lax.rem(visit_z - column + NZ, NZ)
    table[PLACE:STARTS] = place
    table[STARTS:PICK] = starts
    table[PICK:WHICH] = pick
    table[WHICH:] = which

    def spread(values, width, at):
        tap = lax.broadcasted_iota(jnp.int32, (KW, width), 0)
        hot = lax.broadcasted_iota(jnp.int32, (KW, width), 1) == at(tap)
        return jnp.dot(
            values, hot.astype(F32), precision=lax.Precision.HIGHEST, preferred_element_type=F32
        )

    brow[...] = spread(basis_row[...], PIECE, lambda tap: tap + HALO - MARGIN)
    bcol[...] = spread(basis_col[...], OUTW, lambda tap: lax.rem(OUTW - tap, OUTW))


def plan(inter, offset, basis_row, basis_col):
    return pl.pallas_call(
        plan_kernel,
        out_shape=(
            jax.ShapeDtypeStruct((WHICH + 8, KP), jnp.int32),
            jax.ShapeDtypeStruct((NB, PIECE), F32),
            jax.ShapeDtypeStruct((NB, OUTW), F32),
        ),
        in_specs=[pl.BlockSpec(memory_space=pltpu.VMEM)] * 4,
        out_specs=(pl.BlockSpec(memory_space=pltpu.VMEM),) * 3,
        name="plan",
    )(inter, offset, basis_row, basis_col)


def split(x):
    high = x.astype(BF16)
    return high, (x - high.astype(F32)).astype(BF16)


def main_kernel(slots, *refs):
    table, tile_coef, coefs, flux_in, var_in, brow, bcol, conv, var_out = refs[:9]
    ys, yr, zs, zr = (refs[9 + n * NC : 9 + (n + 1) * NC] for n in range(4))
    strips, blocks = refs[9 + 4 * NC : 11 + 4 * NC], refs[11 + 4 * NC : 13 + 4 * NC]
    x_full, x_split, row_band, cb_high, cb_low, rw_high, rw_low = refs[13 + 4 * NC : 20 + 4 * NC]
    in_sem, ys_sem, yr_sem, zs_sem, zr_sem, hs_sem, hr_sem = refs[20 + 4 * NC :]

    me = lax.axis_index("visit")
    tile = lax.axis_index("tile")
    y, z = me // NZ, lax.rem(me, NZ)

    def y_peer(r):
        return (lax.rem(y + r, NY) * NZ + z, tile)

    def z_peer(d):
        return (y * NZ + lax.rem(z + d, NZ), tile)

    def t_peer(s):
        return (me, lax.rem(tile + s + TILES, TILES))

    inputs = [
        pltpu.make_async_copy(source, target, in_sem.at[n])
        for n, (source, target) in enumerate(zip((flux_in, var_in), strips))
    ]
    for copy in inputs:
        copy.start()
    barrier = pltpu.get_barrier_semaphore()
    peers = [y_peer(r) for r in range(1, NY)] + [z_peer(d) for d in range(1, NZ)] + [t_peer(1), t_peer(-1)]
    for peer in peers:
        pl.semaphore_signal(barrier, inc=1, device_id=peer, device_id_type=MESH)
    pl.semaphore_wait(barrier, len(peers))

    def y_copy(c, r):
        return pltpu.make_async_remote_copy(
            src_ref=ys[c].at[pl.ds((r - 1) * PER_ROW, PER_ROW)],
            dst_ref=yr[c].at[pl.ds(r * PER_ROW, PER_ROW)],
            send_sem=ys_sem.at[c, r - 1],
            recv_sem=yr_sem.at[c, r - 1],
            device_id=y_peer(r),
            device_id_type=MESH,
        )

    def z_copy(c, d):
        return pltpu.make_async_remote_copy(
            src_ref=zs[c].at[pl.ds(d * slots, slots)],
            dst_ref=zr[c].at[pl.ds(d * slots, slots)],
            send_sem=zs_sem.at[c, d - 1],
            recv_sem=zr_sem.at[c, d - 1],
            device_id=z_peer(d),
            device_id_type=MESH,
        )

    def halo_copy(which):
        source, target, step = ((TR, 0, 1), (HALO, HALO + TR, -1))[which]
        return pltpu.make_async_remote_copy(
            src_ref=x_full.at[pl.ds(source, HALO)],
            dst_ref=x_full.at[pl.ds(target, HALO)],
            send_sem=hs_sem.at[which],
            recv_sem=hr_sem.at[which],
            device_id=t_peer(step),
            device_id_type=MESH,
        )

    lane = lax.broadcasted_iota(jnp.int32, (CHUNK, PIECE), 1)

    def take_in(plane):
        inputs[plane].wait()

        def one(k, _):
            at = pl.ds(pl.multiple_of(k * PIECE, PIECE), PIECE)
            blocks[plane][k] = strips[plane][:, at]
            return 0

        lax.fori_loop(0, KP, one, 0)

    def cut(c, r, out, first):
        source = blocks[c // PARTS]
        rows = slice(c % PARTS * CHUNK, (c % PARTS + 1) * CHUNK)
        visits = STARTS + lax.rem(y + r, NY) * NZ

        pieces, shifts = [], []
        for vz in range(NZ):
            for j in range(CAP):
                start = table[visits + vz, j]
                block = start // PIECE
                shift = jnp.full((CHUNK, PIECE), start - block * PIECE, jnp.int32)
                here, beside = source[block, rows, :], source[jnp.minimum(block + 1, KP - 1), rows, :]
                pieces.append(jnp.where(lane >= shift, here, beside))
                shifts.append(shift)
        for bit in range(7):
            turned = [pltpu.roll(piece, PIECE - (1 << bit), 1) for piece in pieces]
            pieces = [
                jnp.where((shift & (1 << bit)) != 0, after, piece)
                for shift, after, piece in zip(shifts, turned, pieces)
            ]
        for slot, piece in enumerate(pieces):
            out[first + slot] = piece

    def y_start(c):
        def one(r, _):
            cut(c, r, ys[c], (r - 1) * PER_ROW)
            y_copy(c, r).start()
            return 0

        lax.fori_loop(1, NY, one, 0)
        cut(c, 0, yr[c], 0)

    def forward(c):
        for r in range(1, NY):
            y_copy(c, r).wait_recv()

        def one(e, _):
            half = (e + 1) // 2
            d = NZ // 2 + jnp.where(lax.rem(e, 2) == 1, -half, half)
            row = PICK + y * NZ + lax.rem(z + d, NZ)
            for p in range(slots):
                zs[c][d * slots + p] = yr[c][table[row, p]]
            z_copy(c, d).start()
            return 0

        lax.fori_loop(0, NZ - 1, one, 0)
        for p in range(slots):
            zr[c][p] = yr[c][table[PICK + me, p]]

    def assemble(c, out, row, scale=None):
        for d in range(1, NZ):
            z_copy(c, d).wait_recv()

        def one(k, _):
            piece = zr[c][table[me, k] * slots + table[PLACE + me, k]]
            at = pl.ds(pl.multiple_of(k * PIECE, PIECE), PIECE)
            out[pl.ds(row, CHUNK), at] = piece if scale is None else piece * scale
            return 0

        lax.fori_loop(0, KP, one, 0)

    chosen = tile_coef[me, tile]

    def bands():
        rows = [coefs[chosen, b] * brow[b : b + 1, :] for b in range(NB)]
        for b in range(NB):
            band = pltpu.roll(jnp.broadcast_to(rows[b], (TR, PIECE)), 0, 1, stride=1, stride_axis=0)
            high, low = split(band)
            row_band[b * TR : (b + 1) * TR, 0:PIECE] = high
            row_band[b * TR : (b + 1) * TR, PIECE : 2 * PIECE] = low
            row_band[b * TR : (b + 1) * TR, 2 * PIECE : 3 * PIECE] = high
        whole = lax.dot_general(
            jnp.concatenate(rows, axis=0),
            bcol[...],
            (((0,), (0,)), ((), ())),
            precision=lax.Precision.HIGHEST,
            preferred_element_type=F32,
        )
        def one(b, _):
            line = bcol[pl.ds(b, 1), :]
            for part in range(WIN // 128):
                turned = pltpu.roll(
                    jnp.broadcast_to(line, (128, OUTW)), (part * 128) % OUTW, 1, stride=1, stride_axis=0
                )
                tap = (
                    lax.broadcasted_iota(jnp.int32, (128, OUTW), 0)
                    + part * 128
                    - lax.broadcasted_iota(jnp.int32, (128, OUTW), 1)
                )
                high, low = split(jnp.where((tap >= 0) & (tap < KW), turned, 0.0))
                place = pl.ds(pl.multiple_of(b * WIN + part * 128, 128), 128)
                cb_high[place, :] = high
                cb_low[place, :] = low
            return 0

        lax.fori_loop(0, NB, one, 0)
        return jnp.sum(whole * whole)

    def expand():
        row = lax.broadcasted_iota(jnp.int32, (XROWS, PIECE), 0)
        lane = lax.broadcasted_iota(jnp.int32, (XROWS, PIECE), 1)
        first = jnp.where(tile == 0, HALO, 0)
        last = jnp.where(tile == TILES - 1, HALO + TR, HALO + TR + HALO)
        rows_in = (row >= first) & (row < last)

        def one(j, _):
            here = pl.multiple_of(jnp.minimum(j, KP - 1) * PIECE, PIECE)
            before = pl.multiple_of(jnp.minimum(jnp.maximum(j - 1, 0), KP - 1) * PIECE, PIECE)
            both = jnp.where(
                lane < MARGIN,
                pltpu.roll(x_full[:, pl.ds(before, PIECE)], MARGIN, 1),
                pltpu.roll(x_full[:, pl.ds(here, PIECE)], MARGIN, 1),
            )
            column = j * PIECE + lane - MARGIN
            high, low = split(jnp.where(rows_in & (column >= 0) & (column < WIDTH), both, 0.0))
            place = pl.ds(pl.multiple_of(j * PIECE, PIECE), PIECE)
            x_split[0:XROWS, place] = high
            x_split[XROWS : 2 * XROWS, place] = high
            x_split[2 * XROWS : 3 * XROWS, place] = low
            return 0

        lax.fori_loop(0, XBLOCKS, one, 0)

    def convolve(h):
        def rows(m, _):
            high, low = split(
                jnp.dot(
                    row_band[...],
                    x_split[:, pl.ds(pl.multiple_of((h * HWIN + m) * OUTW, OUTW), OUTW)],
                    preferred_element_type=F32,
                )
            )
            now = pl.ds(pl.multiple_of((m + 1) * TR, TR), TR)
            before = pl.ds(pl.multiple_of(m * TR, TR), TR)
            for out, value in ((rw_high, high), (rw_low, low)):
                for b in range(NB):
                    part = value[b * TR : (b + 1) * TR]
                    out[now, b * WIN : b * WIN + OUTW] = part
                    out[before, b * WIN + OUTW : (b + 1) * WIN] = part[:, 0 : WIN - OUTW]
            return 0

        lax.fori_loop(0, HWIN + 1, rows, 0)
        at = slice(TR, TR + HWIN * TR)
        total = jnp.dot(rw_high[at, :], cb_high[...], preferred_element_type=F32)
        total += jnp.dot(rw_high[at, :], cb_low[...], preferred_element_type=F32)
        total += jnp.dot(rw_low[at, :], cb_high[...], preferred_element_type=F32)
        for n in range(HWIN):
            first = (h * HWIN + n) * OUTW
            conv[:, first : first + OUTW] = total[n * TR : (n + 1) * TR, :]

    take_in(0)
    y_start(0)
    y_start(1)
    y_start(2)
    for c in range(NC):
        forward(c)
        if c + 3 == PARTS:
            take_in(1)
        if c + 3 < NC:
            y_start(c + 3)
        if c == PARTS - 1:
            power = bands()
        if c == NC - 3:
            for part in range(PARTS):
                assemble(part, x_full, HALO + part * CHUNK)
            halo_copy(0).start()
            halo_copy(1).start()
        if c == NC - 2:
            halo_copy(0).wait_recv()
            halo_copy(1).wait_recv()
            expand()
            convolve(0)
    convolve(1)
    for part in range(PARTS):
        assemble(PARTS + part, var_out, part * CHUNK, power)
    halo_copy(0).wait_send()
    halo_copy(1).wait_send()
    for c in range(NC):
        for r in range(1, NY):
            y_copy(c, r).wait_send()
        for d in range(1, NZ):
            z_copy(c, d).wait_send()


def exchange(slots, table, tile_coef, coefs, flux, var, brow, bcol):
    smem = pl.BlockSpec(memory_space=pltpu.SMEM)
    vmem = pl.BlockSpec(memory_space=pltpu.VMEM)
    hbm = pl.BlockSpec(memory_space=pl.ANY)
    scratch = [pltpu.VMEM(((NY - 1) * PER_ROW, CHUNK, PIECE), F32)] * NC
    scratch += [pltpu.VMEM((NY * PER_ROW, CHUNK, PIECE), F32)] * NC
    scratch += [pltpu.VMEM((NZ * slots, CHUNK, PIECE), F32)] * (2 * NC)
    scratch += [
        pltpu.VMEM((TR, WIDTH), F32),
        pltpu.VMEM((TR, WIDTH), F32),
        pltpu.VMEM((KP, TR, PIECE), F32),
        pltpu.VMEM((KP, TR, PIECE), F32),
        pltpu.VMEM((XROWS, WIDTH), F32),
        pltpu.VMEM((3 * XROWS, XBLOCKS * PIECE), BF16),
        pltpu.VMEM((NB * TR, 3 * PIECE), BF16),
        pltpu.VMEM((NB * WIN, OUTW), BF16),
        pltpu.VMEM((NB * WIN, OUTW), BF16),
        pltpu.VMEM(((HWIN + 2) * TR, NB * WIN), BF16),
        pltpu.VMEM(((HWIN + 2) * TR, NB * WIN), BF16),
        pltpu.SemaphoreType.DMA((2,)),
        pltpu.SemaphoreType.DMA((NC, NY - 1)),
        pltpu.SemaphoreType.DMA((NC, NY - 1)),
        pltpu.SemaphoreType.DMA((NC, NZ - 1)),
        pltpu.SemaphoreType.DMA((NC, NZ - 1)),
        pltpu.SemaphoreType.DMA((2,)),
        pltpu.SemaphoreType.DMA((2,)),
    ]
    return pl.pallas_call(
        functools.partial(main_kernel, slots),
        out_shape=(
            jax.ShapeDtypeStruct((TR, WIDTH), F32),
            jax.ShapeDtypeStruct((TR, WIDTH), F32),
        ),
        in_specs=[smem] * 3 + [hbm] * 2 + [vmem] * 2,
        out_specs=(vmem, vmem),
        scratch_shapes=scratch,
        compiler_params=pltpu.CompilerParams(
            collective_id=slots, has_side_effects=True, vmem_limit_bytes=60 << 20
        ),
        cost_estimate=pl.CostEstimate(flops=10**10, bytes_accessed=6 << 20, transcendentals=0),
        name=f"exchange_{slots}",
    )(table, tile_coef, coefs, flux, var, brow, bcol)


def local(
    science,
    science_var,
    template,
    template_var,
    intersection,
    col_offset,
    basis_row,
    basis_col,
    coef_sets,
    tile_coef,
):
    table, brow, bcol = plan(intersection[:, :, 0], col_offset, basis_row, basis_col)
    convolved, variance = lax.switch(
        table[WHICH, 0],
        [functools.partial(exchange, n) for n in VARIANTS],
        table,
        tile_coef,
        coef_sets,
        template[0],
        template_var[0],
        brow,
        bcol,
    )
    return science - convolved[None], science_var + variance[None]


def solution(mesh):
    split3 = P("visit", "tile", None)
    return jax.shard_map(
        local,
        mesh=mesh,
        in_specs=(split3, split3, split3, split3, P(), P(), P(), P(), P(), P()),
        out_specs=(split3, split3),
        check_vma=False,
    )
```

```python
import functools

import jax
import jax.numpy as jnp
from jax import lax
from jax.experimental import pallas as pl
from jax.experimental.pallas import tpu as pltpu
from jax.sharding import PartitionSpec as P

MESH = pl.DeviceIdType.MESH
F32 = jnp.float32
BF16 = jnp.bfloat16

TR = 64
PIECE = 128
KP = 32
KW = 41
MARGIN = 20
NB = 16
NSETS = 8
TILES = 8
WIDTH = 4096
NY = 4
NZ = 8
CAP = 2
PER_ROW = NZ * CAP
CHUNK = 16
PARTS = TR // CHUNK
NC = 2 * PARTS
HALO = 24
XROWS = 128
WIN = 384
OUTW = 256
NWIN = WIDTH // OUTW
XBLOCKS = 34
HALVES = 2
HWIN = NWIN // HALVES
QWIN = HWIN // 2
LAG = 2


PLACE, STARTS, PICK, WHICH = KP, 2 * KP, 3 * KP, 4 * KP
VARIANTS = (5, 6, 8)


def plan_kernel(inter, offset, basis_row, basis_col, table, brow, bcol):
    me = lax.axis_index("visit")
    my_y, my_z = me // NZ, lax.rem(me, NZ)
    owner = inter[...]
    column = lax.rem(owner, NZ)
    lane = lax.broadcasted_iota(jnp.int32, (KP, KP), 1)
    visit_z = lax.rem(lax.broadcasted_iota(jnp.int32, (KP, KP), 0), NZ)
    rank = jnp.zeros((KP, KP), jnp.int32)
    place = jnp.zeros((KP, KP), jnp.int32)
    for k in range(KP - 1):
        later = lane > k
        rank += ((owner == owner[:, k : k + 1]) & later).astype(jnp.int32)
        place += ((column == column[:, k : k + 1]) & later).astype(jnp.int32)
    slot = lax.rem(my_y + NY - owner // NZ, NY) * PER_ROW + visit_z * CAP + rank
    starts = jnp.zeros((KP, KP), jnp.int32)
    for j in range(CAP):
        found = jnp.sum(jnp.where((owner == me) & (rank == j), offset[...], 0), axis=1, keepdims=True)
        starts = jnp.where(lane == j, found, starts)
    pick = jnp.zeros((KP, KP), jnp.int32)
    for p in range(NZ):
        found = jnp.sum(jnp.where((column == my_z) & (place == p), slot, 0), axis=1, keepdims=True)
        pick = jnp.where(lane == p, found, pick)
    most = jnp.max(place) + 1
    which = jnp.zeros((8, KP), jnp.int32)
    for n in VARIANTS[:-1]:
        which += (most > n).astype(jnp.int32)
    table[0:PLACE] = lax.rem(visit_z - column + NZ, NZ)
    table[PLACE:STARTS] = place
    table[STARTS:PICK] = starts
    table[PICK:WHICH] = pick
    table[WHICH:] = which

    def spread(values, width, at):
        tap = lax.broadcasted_iota(jnp.int32, (KW, width), 0)
        hot = lax.broadcasted_iota(jnp.int32, (KW, width), 1) == at(tap)
        return jnp.dot(
            values, hot.astype(F32), precision=lax.Precision.HIGHEST, preferred_element_type=F32
        )

    brow[...] = spread(basis_row[...], PIECE, lambda tap: tap + HALO - MARGIN)
    bcol[...] = spread(basis_col[...], OUTW, lambda tap: lax.rem(OUTW - tap, OUTW))


def plan(inter, offset, basis_row, basis_col):
    return pl.pallas_call(
        plan_kernel,
        out_shape=(
            jax.ShapeDtypeStruct((WHICH + 8, KP), jnp.int32),
            jax.ShapeDtypeStruct((NB, PIECE), F32),
            jax.ShapeDtypeStruct((NB, OUTW), F32),
        ),
        in_specs=[pl.BlockSpec(memory_space=pltpu.VMEM)] * 4,
        out_specs=(pl.BlockSpec(memory_space=pltpu.VMEM),) * 3,
        name="plan",
    )(inter, offset, basis_row, basis_col)


def split(x):
    high = x.astype(BF16)
    return high, (x - high.astype(F32)).astype(BF16)


def main_kernel(slots, *refs):
    table, tile_coef, coefs, flux_in, var_in, brow, bcol, conv, var_out = refs[:9]
    yr, zs, zr = (refs[9 + n * NC : 9 + (n + 1) * NC] for n in range(3))
    ys, flux_strip, var_strip, blocks, power = refs[9 + 3 * NC : 14 + 3 * NC]
    x_full, x_split, row_band, cb_high, cb_low, rw_high, rw_low = refs[14 + 3 * NC : 21 + 3 * NC]
    in_sem, own_sem, ys_sem, yr_sem, zs_sem, zr_sem, hs_sem, hr_sem = refs[21 + 3 * NC :]
    strips = (flux_strip, var_strip)

    me = lax.axis_index("visit")
    tile = lax.axis_index("tile")
    y, z = me // NZ, lax.rem(me, NZ)

    def y_peer(r):
        return (lax.rem(y + r, NY) * NZ + z, tile)

    def z_peer(d):
        return (y * NZ + lax.rem(z + d, NZ), tile)

    def t_peer(s):
        return (me, lax.rem(tile + s + TILES, TILES))

    inputs = [
        pltpu.make_async_copy(source, target, in_sem.at[n])
        for n, (source, target) in enumerate(zip((flux_in, var_in), strips))
    ]
    for copy in inputs:
        copy.start()
    barrier = pltpu.get_barrier_semaphore()
    peers = [y_peer(r) for r in range(1, NY)] + [z_peer(d) for d in range(1, NZ)] + [t_peer(1), t_peer(-1)]
    for peer in peers:
        pl.semaphore_signal(barrier, inc=1, device_id=peer, device_id_type=MESH)
    pl.semaphore_wait(barrier, len(peers))

    def y_copy(c, r):
        return pltpu.make_async_remote_copy(
            src_ref=ys.at[pl.ds((c * NY + r) * PER_ROW, PER_ROW)],
            dst_ref=yr[c].at[pl.ds(r * PER_ROW, PER_ROW)],
            send_sem=ys_sem.at[c, r - 1],
            recv_sem=yr_sem.at[c, r - 1],
            device_id=y_peer(r),
            device_id_type=MESH,
        )

    def own_copy(c):
        return pltpu.make_async_copy(
            ys.at[pl.ds(c * NY * PER_ROW, PER_ROW)], yr[c].at[pl.ds(0, PER_ROW)], own_sem.at[c]
        )

    def z_copy(c, d):
        return pltpu.make_async_remote_copy(
            src_ref=zs[c].at[pl.ds(d * slots, slots)],
            dst_ref=zr[c].at[pl.ds(d * slots, slots)],
            send_sem=zs_sem.at[c, d - 1],
            recv_sem=zr_sem.at[c, d - 1],
            device_id=z_peer(d),
            device_id_type=MESH,
        )

    def halo_copy(which):
        source, target, step = ((TR, 0, 1), (HALO, HALO + TR, -1))[which]
        return pltpu.make_async_remote_copy(
            src_ref=x_full.at[pl.ds(source, HALO)],
            dst_ref=x_full.at[pl.ds(target, HALO)],
            send_sem=hs_sem.at[which],
            recv_sem=hr_sem.at[which],
            device_id=t_peer(step),
            device_id_type=MESH,
        )

    lane = lax.broadcasted_iota(jnp.int32, (CHUNK, PIECE), 1)

    def take_in(plane):
        inputs[plane].wait()

        def one(k, _):
            at = pl.ds(pl.multiple_of(k * PIECE, PIECE), PIECE)
            blocks[plane * KP + k] = strips[plane][:, at]
            return 0

        lax.fori_loop(0, KP, one, 0)

    def cut(c):
        first = c // PARTS * KP
        rows = pl.ds(pl.multiple_of(lax.rem(c, PARTS) * CHUNK, CHUNK), CHUNK)

        def one(r, _):
            visits = STARTS + lax.rem(y + r, NY) * NZ
            pieces, shifts = [], []
            for vz in range(NZ):
                for j in range(CAP):
                    start = table[visits + vz, j]
                    block = start // PIECE
                    shift = jnp.full((CHUNK, PIECE), start - block * PIECE, jnp.int32)
                    here = blocks[first + block, rows, :]
                    beside = blocks[first + jnp.minimum(block + 1, KP - 1), rows, :]
                    pieces.append(jnp.where(lane >= shift, here, beside))
                    shifts.append(shift)
            for bit in range(7):
                turned = [pltpu.roll(piece, PIECE - (1 << bit), 1) for piece in pieces]
                pieces = [
                    jnp.where((shift & (1 << bit)) != 0, after, piece)
                    for shift, after, piece in zip(shifts, turned, pieces)
                ]
            for slot, piece in enumerate(pieces):
                ys[(c * NY + r) * PER_ROW + slot] = piece
            return 0

        lax.fori_loop(0, NY, one, 0)

    def y_start(c):
        for r in (2, 1, 3):
            y_copy(c, r).start()
        own_copy(c).start()

    def forward(c):
        own_copy(c).wait()
        for r in range(1, NY):
            y_copy(c, r).wait_recv()

        def one(e, _):
            half = (e + 1) // 2
            d = NZ // 2 + jnp.where(lax.rem(e, 2) == 1, -half, half)
            row = PICK + y * NZ + lax.rem(z + d, NZ)
            for p in range(slots):
                zs[c][d * slots + p] = yr[c][table[row, p]]
            z_copy(c, d).start()
            return 0

        lax.fori_loop(0, NZ - 1, one, 0)
        for p in range(slots):
            zr[c][p] = yr[c][table[PICK + me, p]]

    def assemble(c, out, row, scale=None):
        for d in range(1, NZ):
            z_copy(c, d).wait_recv()

        def one(k, _):
            piece = zr[c][table[me, k] * slots + table[PLACE + me, k]]
            at = pl.ds(pl.multiple_of(k * PIECE, PIECE), PIECE)
            out[pl.ds(row, CHUNK), at] = piece if scale is None else piece * scale
            return 0

        lax.fori_loop(0, KP, one, 0)

    chosen = tile_coef[me, tile]

    def bands():
        rows = [coefs[chosen, b] * brow[b : b + 1, :] for b in range(NB)]
        for b in range(NB):
            band = pltpu.roll(jnp.broadcast_to(rows[b], (TR, PIECE)), 0, 1, stride=1, stride_axis=0)
            high, low = split(band)
            row_band[b * TR : (b + 1) * TR, 0:PIECE] = high
            row_band[b * TR : (b + 1) * TR, PIECE : 2 * PIECE] = low
            row_band[b * TR : (b + 1) * TR, 2 * PIECE : 3 * PIECE] = high
        whole = lax.dot_general(
            jnp.concatenate(rows, axis=0),
            bcol[...],
            (((0,), (0,)), ((), ())),
            precision=lax.Precision.HIGHEST,
            preferred_element_type=F32,
        )
        def one(b, _):
            line = bcol[pl.ds(b, 1), :]
            for part in range(WIN // 128):
                turned = pltpu.roll(
                    jnp.broadcast_to(line, (128, OUTW)), (part * 128) % OUTW, 1, stride=1, stride_axis=0
                )
                tap = (
                    lax.broadcasted_iota(jnp.int32, (128, OUTW), 0)
                    + part * 128
                    - lax.broadcasted_iota(jnp.int32, (128, OUTW), 1)
                )
                high, low = split(jnp.where((tap >= 0) & (tap < KW), turned, 0.0))
                place = pl.ds(pl.multiple_of(b * WIN + part * 128, 128), 128)
                cb_high[place, :] = high
                cb_low[place, :] = low
            return 0

        lax.fori_loop(0, NB, one, 0)
        power[0] = jnp.sum(whole * whole)

    def expand():
        row = lax.broadcasted_iota(jnp.int32, (XROWS, PIECE), 0)
        lane = lax.broadcasted_iota(jnp.int32, (XROWS, PIECE), 1)
        first = jnp.where(tile == 0, HALO, 0)
        last = jnp.where(tile == TILES - 1, HALO + TR, HALO + TR + HALO)
        rows_in = (row >= first) & (row < last)

        def one(j, _):
            here = pl.multiple_of(jnp.minimum(j, KP - 1) * PIECE, PIECE)
            before = pl.multiple_of(jnp.minimum(jnp.maximum(j - 1, 0), KP - 1) * PIECE, PIECE)
            both = jnp.where(
                lane < MARGIN,
                pltpu.roll(x_full[:, pl.ds(before, PIECE)], MARGIN, 1),
                pltpu.roll(x_full[:, pl.ds(here, PIECE)], MARGIN, 1),
            )
            column = j * PIECE + lane - MARGIN
            high, low = split(jnp.where(rows_in & (column >= 0) & (column < WIDTH), both, 0.0))
            place = pl.ds(pl.multiple_of(j * PIECE, PIECE), PIECE)
            x_split[0:XROWS, place] = high
            x_split[XROWS : 2 * XROWS, place] = high
            x_split[2 * XROWS : 3 * XROWS, place] = low
            return 0

        lax.fori_loop(0, XBLOCKS, one, 0)

    def convolve(h, _):
        def rows(m, _):
            high, low = split(
                jnp.dot(
                    row_band[...],
                    x_split[:, pl.ds(pl.multiple_of((h * HWIN + m) * OUTW, OUTW), OUTW)],
                    preferred_element_type=F32,
                )
            )
            now = pl.ds(pl.multiple_of((m + 1) * TR, TR), TR)
            before = pl.ds(pl.multiple_of(m * TR, TR), TR)
            for out, value in ((rw_high, high), (rw_low, low)):
                for b in range(NB):
                    part = value[b * TR : (b + 1) * TR]
                    out[now, b * WIN : b * WIN + OUTW] = part
                    out[before, b * WIN + OUTW : (b + 1) * WIN] = part[:, 0 : WIN - OUTW]
            return 0

        def cols(q, _):
            at = pl.ds(pl.multiple_of(TR + q * QWIN * TR, TR), QWIN * TR)
            total = jnp.dot(rw_high[at, :], cb_high[...], preferred_element_type=F32)
            total += jnp.dot(rw_high[at, :], cb_low[...], preferred_element_type=F32)
            total += jnp.dot(rw_low[at, :], cb_high[...], preferred_element_type=F32)
            for n in range(QWIN):
                first = pl.multiple_of((h * HWIN + q * QWIN + n) * OUTW, OUTW)
                conv[:, pl.ds(first, OUTW)] = total[n * TR : (n + 1) * TR, :]
            return 0

        lax.fori_loop(0, HWIN + 1, rows, 0)
        lax.fori_loop(0, HWIN // QWIN, cols, 0)
        return 0

    def step(i, _):
        @pl.when(i < NC)
        def _():
            cut(i)

        for c in range(NC):

            @pl.when(i == c)
            def _():
                y_start(c)

        @pl.when(i == PARTS - 1)
        def _():
            take_in(1)

        for c in range(NC):

            @pl.when(i == c + LAG)
            def _():
                forward(c)

        @pl.when(i == PARTS - 1 + LAG)
        def _():
            bands()

        @pl.when(i == NC - 3 + LAG)
        def _():
            for part in range(PARTS):
                assemble(part, x_full, HALO + part * CHUNK)
            halo_copy(0).start()
            halo_copy(1).start()

        return 0

    take_in(0)
    lax.fori_loop(0, NC + LAG, step, 0)
    halo_copy(0).wait_recv()
    halo_copy(1).wait_recv()
    expand()
    lax.fori_loop(0, HALVES, convolve, 0)
    for part in range(PARTS):
        assemble(PARTS + part, var_out, part * CHUNK, power[0])
    halo_copy(0).wait_send()
    halo_copy(1).wait_send()
    for c in range(NC):
        for r in range(1, NY):
            y_copy(c, r).wait_send()
        for d in range(1, NZ):
            z_copy(c, d).wait_send()


def exchange(slots, table, tile_coef, coefs, flux, var, brow, bcol):
    smem = pl.BlockSpec(memory_space=pltpu.SMEM)
    vmem = pl.BlockSpec(memory_space=pltpu.VMEM)
    hbm = pl.BlockSpec(memory_space=pl.ANY)
    scratch = [pltpu.VMEM((NY * PER_ROW, CHUNK, PIECE), F32)] * NC
    scratch += [pltpu.VMEM((NZ * slots, CHUNK, PIECE), F32)] * (2 * NC)
    scratch += [
        pltpu.VMEM((NC * NY * PER_ROW, CHUNK, PIECE), F32),
        pltpu.VMEM((TR, WIDTH), F32),
        pltpu.VMEM((TR, WIDTH), F32),
        pltpu.VMEM((2 * KP, TR, PIECE), F32),
        pltpu.SMEM((1,), F32),
        pltpu.VMEM((XROWS, WIDTH), F32),
        pltpu.VMEM((3 * XROWS, XBLOCKS * PIECE), BF16),
        pltpu.VMEM((NB * TR, 3 * PIECE), BF16),
        pltpu.VMEM((NB * WIN, OUTW), BF16),
        pltpu.VMEM((NB * WIN, OUTW), BF16),
        pltpu.VMEM(((HWIN + 2) * TR, NB * WIN), BF16),
        pltpu.VMEM(((HWIN + 2) * TR, NB * WIN), BF16),
        pltpu.SemaphoreType.DMA((2,)),
        pltpu.SemaphoreType.DMA((NC,)),
        pltpu.SemaphoreType.DMA((NC, NY - 1)),
        pltpu.SemaphoreType.DMA((NC, NY - 1)),
        pltpu.SemaphoreType.DMA((NC, NZ - 1)),
        pltpu.SemaphoreType.DMA((NC, NZ - 1)),
        pltpu.SemaphoreType.DMA((2,)),
        pltpu.SemaphoreType.DMA((2,)),
    ]
    return pl.pallas_call(
        functools.partial(main_kernel, slots),
        out_shape=(
            jax.ShapeDtypeStruct((TR, WIDTH), F32),
            jax.ShapeDtypeStruct((TR, WIDTH), F32),
        ),
        in_specs=[smem] * 3 + [hbm] * 2 + [vmem] * 2,
        out_specs=(vmem, vmem),
        scratch_shapes=scratch,
        compiler_params=pltpu.CompilerParams(
            collective_id=slots, has_side_effects=True, vmem_limit_bytes=60 << 20
        ),
        cost_estimate=pl.CostEstimate(flops=10**10, bytes_accessed=6 << 20, transcendentals=0),
        name=f"exchange_{slots}",
    )(table, tile_coef, coefs, flux, var, brow, bcol)


def local(
    science,
    science_var,
    template,
    template_var,
    intersection,
    col_offset,
    basis_row,
    basis_col,
    coef_sets,
    tile_coef,
):
    table, brow, bcol = plan(intersection[:, :, 0], col_offset, basis_row, basis_col)
    convolved, variance = lax.switch(
        table[WHICH, 0],
        [functools.partial(exchange, n) for n in VARIANTS],
        table,
        tile_coef,
        coef_sets,
        template[0],
        template_var[0],
        brow,
        bcol,
    )
    return science - convolved[None], science_var + variance[None]


def solution(mesh):
    split3 = P("visit", "tile", None)
    return jax.shard_map(
        local,
        mesh=mesh,
        in_specs=(split3, split3, split3, split3, P(), P(), P(), P(), P(), P()),
        out_specs=(split3, split3),
        check_vma=False,
    )
```

```python
import functools

import jax
import jax.numpy as jnp
from jax import lax
from jax.experimental import pallas as pl
from jax.experimental.pallas import tpu as pltpu
from jax.sharding import PartitionSpec as P

MESH = pl.DeviceIdType.MESH
F32 = jnp.float32
BF16 = jnp.bfloat16

TR = 64
PIECE = 128
KP = 32
KW = 41
MARGIN = 20
NB = 16
NSETS = 8
TILES = 8
WIDTH = 4096
NY = 4
NZ = 8
CAP = 2
PER_ROW = NZ * CAP
CHUNK = 32
PARTS = TR // CHUNK
NC = 2 * PARTS
HALO = 24
XROWS = 128
WIN = 384
OUTW = 256
NWIN = WIDTH // OUTW
XBLOCKS = 34
HALVES = 2
HWIN = NWIN // HALVES
QWIN = HWIN // 2
LAG = 2


PLACE, STARTS, PICK, WHICH = KP, 2 * KP, 3 * KP, 4 * KP
VARIANTS = (5, 6, 8)


def plan_kernel(inter, offset, basis_row, basis_col, table, brow, bcol):
    me = lax.axis_index("visit")
    my_y, my_z = me // NZ, lax.rem(me, NZ)
    owner = inter[...]
    column = lax.rem(owner, NZ)
    lane = lax.broadcasted_iota(jnp.int32, (KP, KP), 1)
    visit_z = lax.rem(lax.broadcasted_iota(jnp.int32, (KP, KP), 0), NZ)
    rank = jnp.zeros((KP, KP), jnp.int32)
    place = jnp.zeros((KP, KP), jnp.int32)
    for k in range(KP - 1):
        later = lane > k
        rank += ((owner == owner[:, k : k + 1]) & later).astype(jnp.int32)
        place += ((column == column[:, k : k + 1]) & later).astype(jnp.int32)
    slot = lax.rem(my_y + NY - owner // NZ, NY) * PER_ROW + visit_z * CAP + rank
    starts = jnp.zeros((KP, KP), jnp.int32)
    for j in range(CAP):
        found = jnp.sum(jnp.where((owner == me) & (rank == j), offset[...], 0), axis=1, keepdims=True)
        starts = jnp.where(lane == j, found, starts)
    pick = jnp.zeros((KP, KP), jnp.int32)
    for p in range(NZ):
        found = jnp.sum(jnp.where((column == my_z) & (place == p), slot, 0), axis=1, keepdims=True)
        pick = jnp.where(lane == p, found, pick)
    most = jnp.max(place) + 1
    which = jnp.zeros((8, KP), jnp.int32)
    for n in VARIANTS[:-1]:
        which += (most > n).astype(jnp.int32)
    table[0:PLACE] = lax.rem(visit_z - column + NZ, NZ)
    table[PLACE:STARTS] = place
    table[STARTS:PICK] = starts
    table[PICK:WHICH] = pick
    table[WHICH:] = which

    def spread(values, width, at):
        tap = lax.broadcasted_iota(jnp.int32, (KW, width), 0)
        hot = lax.broadcasted_iota(jnp.int32, (KW, width), 1) == at(tap)
        return jnp.dot(
            values, hot.astype(F32), precision=lax.Precision.HIGHEST, preferred_element_type=F32
        )

    brow[...] = spread(basis_row[...], PIECE, lambda tap: tap + HALO - MARGIN)
    bcol[...] = spread(basis_col[...], OUTW, lambda tap: lax.rem(OUTW - tap, OUTW))


def plan(inter, offset, basis_row, basis_col):
    return pl.pallas_call(
        plan_kernel,
        out_shape=(
            jax.ShapeDtypeStruct((WHICH + 8, KP), jnp.int32),
            jax.ShapeDtypeStruct((NB, PIECE), F32),
            jax.ShapeDtypeStruct((NB, OUTW), F32),
        ),
        in_specs=[pl.BlockSpec(memory_space=pltpu.VMEM)] * 4,
        out_specs=(pl.BlockSpec(memory_space=pltpu.VMEM),) * 3,
        name="plan",
    )(inter, offset, basis_row, basis_col)


def split(x):
    high = x.astype(BF16)
    return high, (x - high.astype(F32)).astype(BF16)


def main_kernel(slots, *refs):
    table, tile_coef, coefs, flux_in, var_in, brow, bcol, conv, var_out = refs[:9]
    yr, zs, zr = (refs[9 + n * NC : 9 + (n + 1) * NC] for n in range(3))
    ys, flux_strip, var_strip, blocks, power = refs[9 + 3 * NC : 14 + 3 * NC]
    x_full, x_split, row_band, cb_high, cb_low, rw_high, rw_low = refs[14 + 3 * NC : 21 + 3 * NC]
    in_sem, own_sem, ys_sem, yr_sem, zs_sem, zr_sem, hs_sem, hr_sem = refs[21 + 3 * NC :]
    strips = (flux_strip, var_strip)

    me = lax.axis_index("visit")
    tile = lax.axis_index("tile")
    y, z = me // NZ, lax.rem(me, NZ)

    def y_peer(r):
        return (lax.rem(y + r, NY) * NZ + z, tile)

    def z_peer(d):
        return (y * NZ + lax.rem(z + d, NZ), tile)

    def t_peer(s):
        return (me, lax.rem(tile + s + TILES, TILES))

    inputs = [
        pltpu.make_async_copy(source, target, in_sem.at[n])
        for n, (source, target) in enumerate(zip((flux_in, var_in), strips))
    ]
    for copy in inputs:
        copy.start()
    barrier = pltpu.get_barrier_semaphore()
    peers = [y_peer(r) for r in range(1, NY)] + [z_peer(d) for d in range(1, NZ)] + [t_peer(1), t_peer(-1)]
    for peer in peers:
        pl.semaphore_signal(barrier, inc=1, device_id=peer, device_id_type=MESH)
    pl.semaphore_wait(barrier, len(peers))

    def y_copy(c, r):
        return pltpu.make_async_remote_copy(
            src_ref=ys.at[pl.ds((c * NY + r) * PER_ROW, PER_ROW)],
            dst_ref=yr[c].at[pl.ds(r * PER_ROW, PER_ROW)],
            send_sem=ys_sem.at[c, r - 1],
            recv_sem=yr_sem.at[c, r - 1],
            device_id=y_peer(r),
            device_id_type=MESH,
        )

    def own_copy(c):
        return pltpu.make_async_copy(
            ys.at[pl.ds(c * NY * PER_ROW, PER_ROW)], yr[c].at[pl.ds(0, PER_ROW)], own_sem.at[c]
        )

    def z_copy(c, d):
        return pltpu.make_async_remote_copy(
            src_ref=zs[c].at[pl.ds(d * slots, slots)],
            dst_ref=zr[c].at[pl.ds(d * slots, slots)],
            send_sem=zs_sem.at[c, d - 1],
            recv_sem=zr_sem.at[c, d - 1],
            device_id=z_peer(d),
            device_id_type=MESH,
        )

    def halo_copy(which):
        source, target, step = ((TR, 0, 1), (HALO, HALO + TR, -1))[which]
        return pltpu.make_async_remote_copy(
            src_ref=x_full.at[pl.ds(source, HALO)],
            dst_ref=x_full.at[pl.ds(target, HALO)],
            send_sem=hs_sem.at[which],
            recv_sem=hr_sem.at[which],
            device_id=t_peer(step),
            device_id_type=MESH,
        )

    lane = lax.broadcasted_iota(jnp.int32, (CHUNK, PIECE), 1)

    def take_in(plane):
        inputs[plane].wait()

        def one(k, _):
            at = pl.ds(pl.multiple_of(k * PIECE, PIECE), PIECE)
            blocks[plane * KP + k] = strips[plane][:, at]
            return 0

        lax.fori_loop(0, KP, one, 0)

    def cut(c):
        first = c // PARTS * KP
        rows = pl.ds(pl.multiple_of(lax.rem(c, PARTS) * CHUNK, CHUNK), CHUNK)

        def one(r, _):
            visits = STARTS + lax.rem(y + r, NY) * NZ
            pieces, shifts = [], []
            for vz in range(NZ):
                for j in range(CAP):
                    start = table[visits + vz, j]
                    block = start // PIECE
                    shift = jnp.full((CHUNK, PIECE), start - block * PIECE, jnp.int32)
                    here = blocks[first + block, rows, :]
                    beside = blocks[first + jnp.minimum(block + 1, KP - 1), rows, :]
                    pieces.append(jnp.where(lane >= shift, here, beside))
                    shifts.append(shift)
            for bit in range(7):
                turned = [pltpu.roll(piece, PIECE - (1 << bit), 1) for piece in pieces]
                pieces = [
                    jnp.where((shift & (1 << bit)) != 0, after, piece)
                    for shift, after, piece in zip(shifts, turned, pieces)
                ]
            for slot, piece in enumerate(pieces):
                ys[(c * NY + r) * PER_ROW + slot] = piece
            return 0

        lax.fori_loop(0, NY, one, 0)

    def y_start(c):
        for r in (2, 1, 3):
            y_copy(c, r).start()
        own_copy(c).start()

    def forward(c):
        own_copy(c).wait()
        for r in range(1, NY):
            y_copy(c, r).wait_recv()

        def one(e, _):
            half = (e + 1) // 2
            d = NZ // 2 + jnp.where(lax.rem(e, 2) == 1, -half, half)
            row = PICK + y * NZ + lax.rem(z + d, NZ)
            for p in range(slots):
                zs[c][d * slots + p] = yr[c][table[row, p]]
            z_copy(c, d).start()
            return 0

        lax.fori_loop(0, NZ - 1, one, 0)
        for p in range(slots):
            zr[c][p] = yr[c][table[PICK + me, p]]

    def assemble(c, out, row, scale=None):
        for d in range(1, NZ):
            z_copy(c, d).wait_recv()

        def one(k, _):
            piece = zr[c][table[me, k] * slots + table[PLACE + me, k]]
            at = pl.ds(pl.multiple_of(k * PIECE, PIECE), PIECE)
            out[pl.ds(row, CHUNK), at] = piece if scale is None else piece * scale
            return 0

        lax.fori_loop(0, KP, one, 0)

    chosen = tile_coef[me, tile]

    def bands():
        rows = [coefs[chosen, b] * brow[b : b + 1, :] for b in range(NB)]
        for b in range(NB):
            band = pltpu.roll(jnp.broadcast_to(rows[b], (TR, PIECE)), 0, 1, stride=1, stride_axis=0)
            high, low = split(band)
            row_band[b * TR : (b + 1) * TR, 0:PIECE] = high
            row_band[b * TR : (b + 1) * TR, PIECE : 2 * PIECE] = low
            row_band[b * TR : (b + 1) * TR, 2 * PIECE : 3 * PIECE] = high
        whole = lax.dot_general(
            jnp.concatenate(rows, axis=0),
            bcol[...],
            (((0,), (0,)), ((), ())),
            precision=lax.Precision.HIGHEST,
            preferred_element_type=F32,
        )
        def one(b, _):
            line = bcol[pl.ds(b, 1), :]
            for part in range(WIN // 128):
                turned = pltpu.roll(
                    jnp.broadcast_to(line, (128, OUTW)), (part * 128) % OUTW, 1, stride=1, stride_axis=0
                )
                tap = (
                    lax.broadcasted_iota(jnp.int32, (128, OUTW), 0)
                    + part * 128
                    - lax.broadcasted_iota(jnp.int32, (128, OUTW), 1)
                )
                high, low = split(jnp.where((tap >= 0) & (tap < KW), turned, 0.0))
                place = pl.ds(pl.multiple_of(b * WIN + part * 128, 128), 128)
                cb_high[place, :] = high
                cb_low[place, :] = low
            return 0

        lax.fori_loop(0, NB, one, 0)
        power[0] = jnp.sum(whole * whole)

    def expand():
        row = lax.broadcasted_iota(jnp.int32, (XROWS, PIECE), 0)
        lane = lax.broadcasted_iota(jnp.int32, (XROWS, PIECE), 1)
        first = jnp.where(tile == 0, HALO, 0)
        last = jnp.where(tile == TILES - 1, HALO + TR, HALO + TR + HALO)
        rows_in = (row >= first) & (row < last)

        def one(j, _):
            here = pl.multiple_of(jnp.minimum(j, KP - 1) * PIECE, PIECE)
            before = pl.multiple_of(jnp.minimum(jnp.maximum(j - 1, 0), KP - 1) * PIECE, PIECE)
            both = jnp.where(
                lane < MARGIN,
                pltpu.roll(x_full[:, pl.ds(before, PIECE)], MARGIN, 1),
                pltpu.roll(x_full[:, pl.ds(here, PIECE)], MARGIN, 1),
            )
            column = j * PIECE + lane - MARGIN
            high, low = split(jnp.where(rows_in & (column >= 0) & (column < WIDTH), both, 0.0))
            place = pl.ds(pl.multiple_of(j * PIECE, PIECE), PIECE)
            x_split[0:XROWS, place] = high
            x_split[XROWS : 2 * XROWS, place] = high
            x_split[2 * XROWS : 3 * XROWS, place] = low
            return 0

        lax.fori_loop(0, XBLOCKS, one, 0)

    def convolve(h):
        def rows(m, _):
            high, low = split(
                jnp.dot(
                    row_band[...],
                    x_split[:, pl.ds(pl.multiple_of((h * HWIN + m) * OUTW, OUTW), OUTW)],
                    preferred_element_type=F32,
                )
            )
            now = pl.ds(pl.multiple_of((m + 1) * TR, TR), TR)
            before = pl.ds(pl.multiple_of(m * TR, TR), TR)
            for out, value in ((rw_high, high), (rw_low, low)):
                for b in range(NB):
                    part = value[b * TR : (b + 1) * TR]
                    out[now, b * WIN : b * WIN + OUTW] = part
                    out[before, b * WIN + OUTW : (b + 1) * WIN] = part[:, 0 : WIN - OUTW]
            return 0

        def cols(q, _):
            at = pl.ds(pl.multiple_of(TR + q * QWIN * TR, TR), QWIN * TR)
            total = jnp.dot(rw_high[at, :], cb_high[...], preferred_element_type=F32)
            total += jnp.dot(rw_high[at, :], cb_low[...], preferred_element_type=F32)
            total += jnp.dot(rw_low[at, :], cb_high[...], preferred_element_type=F32)
            for n in range(QWIN):
                first = pl.multiple_of((h * HWIN + q * QWIN + n) * OUTW, OUTW)
                conv[:, pl.ds(first, OUTW)] = total[n * TR : (n + 1) * TR, :]
            return 0

        lax.fori_loop(0, HWIN + 1, rows, 0)
        lax.fori_loop(0, HWIN // QWIN, cols, 0)

    def step(i, _):
        @pl.when(i < NC)
        def _():
            cut(i)

        for c in range(NC):

            @pl.when(i == c)
            def _():
                y_start(c)

        @pl.when(i == PARTS - 1)
        def _():
            take_in(1)

        for c in range(NC):

            @pl.when(i == c + LAG)
            def _():
                forward(c)

        @pl.when(i == PARTS - 1 + LAG)
        def _():
            bands()

        @pl.when(i == NC - 3 + LAG)
        def _():
            for part in range(PARTS):
                assemble(part, x_full, HALO + part * CHUNK)
            halo_copy(0).start()
            halo_copy(1).start()

        @pl.when(i == NC - HALVES + LAG)
        def _():
            halo_copy(0).wait_recv()
            halo_copy(1).wait_recv()
            expand()

        @pl.when(i >= NC - HALVES + LAG)
        def _():
            convolve(i - (NC - HALVES + LAG))

        return 0

    take_in(0)
    lax.fori_loop(0, NC + LAG, step, 0)
    for part in range(PARTS):
        assemble(PARTS + part, var_out, part * CHUNK, power[0])
    halo_copy(0).wait_send()
    halo_copy(1).wait_send()
    for c in range(NC):
        for r in range(1, NY):
            y_copy(c, r).wait_send()
        for d in range(1, NZ):
            z_copy(c, d).wait_send()


def exchange(slots, table, tile_coef, coefs, flux, var, brow, bcol):
    smem = pl.BlockSpec(memory_space=pltpu.SMEM)
    vmem = pl.BlockSpec(memory_space=pltpu.VMEM)
    hbm = pl.BlockSpec(memory_space=pl.ANY)
    scratch = [pltpu.VMEM((NY * PER_ROW, CHUNK, PIECE), F32)] * NC
    scratch += [pltpu.VMEM((NZ * slots, CHUNK, PIECE), F32)] * (2 * NC)
    scratch += [
        pltpu.VMEM((NC * NY * PER_ROW, CHUNK, PIECE), F32),
        pltpu.VMEM((TR, WIDTH), F32),
        pltpu.VMEM((TR, WIDTH), F32),
        pltpu.VMEM((2 * KP, TR, PIECE), F32),
        pltpu.SMEM((1,), F32),
        pltpu.VMEM((XROWS, WIDTH), F32),
        pltpu.VMEM((3 * XROWS, XBLOCKS * PIECE), BF16),
        pltpu.VMEM((NB * TR, 3 * PIECE), BF16),
        pltpu.VMEM((NB * WIN, OUTW), BF16),
        pltpu.VMEM((NB * WIN, OUTW), BF16),
        pltpu.VMEM(((HWIN + 2) * TR, NB * WIN), BF16),
        pltpu.VMEM(((HWIN + 2) * TR, NB * WIN), BF16),
        pltpu.SemaphoreType.DMA((2,)),
        pltpu.SemaphoreType.DMA((NC,)),
        pltpu.SemaphoreType.DMA((NC, NY - 1)),
        pltpu.SemaphoreType.DMA((NC, NY - 1)),
        pltpu.SemaphoreType.DMA((NC, NZ - 1)),
        pltpu.SemaphoreType.DMA((NC, NZ - 1)),
        pltpu.SemaphoreType.DMA((2,)),
        pltpu.SemaphoreType.DMA((2,)),
    ]
    return pl.pallas_call(
        functools.partial(main_kernel, slots),
        out_shape=(
            jax.ShapeDtypeStruct((TR, WIDTH), F32),
            jax.ShapeDtypeStruct((TR, WIDTH), F32),
        ),
        in_specs=[smem] * 3 + [hbm] * 2 + [vmem] * 2,
        out_specs=(vmem, vmem),
        scratch_shapes=scratch,
        compiler_params=pltpu.CompilerParams(
            collective_id=slots, has_side_effects=True, vmem_limit_bytes=60 << 20
        ),
        cost_estimate=pl.CostEstimate(flops=10**10, bytes_accessed=6 << 20, transcendentals=0),
        name=f"exchange_{slots}",
    )(table, tile_coef, coefs, flux, var, brow, bcol)


def local(
    science,
    science_var,
    template,
    template_var,
    intersection,
    col_offset,
    basis_row,
    basis_col,
    coef_sets,
    tile_coef,
):
    table, brow, bcol = plan(intersection[:, :, 0], col_offset, basis_row, basis_col)
    convolved, variance = lax.switch(
        table[WHICH, 0],
        [functools.partial(exchange, n) for n in VARIANTS],
        table,
        tile_coef,
        coef_sets,
        template[0],
        template_var[0],
        brow,
        bcol,
    )
    return science - convolved[None], science_var + variance[None]


def solution(mesh):
    split3 = P("visit", "tile", None)
    return jax.shard_map(
        local,
        mesh=mesh,
        in_specs=(split3, split3, split3, split3, P(), P(), P(), P(), P(), P()),
        out_specs=(split3, split3),
        check_vma=False,
    )
```

```python
import functools

import jax
import jax.numpy as jnp
from jax import lax
from jax.experimental import pallas as pl
from jax.experimental.pallas import tpu as pltpu
from jax.sharding import PartitionSpec as P

MESH = pl.DeviceIdType.MESH
F32 = jnp.float32
BF16 = jnp.bfloat16

TR = 64
PIECE = 128
KP = 32
KW = 41
MARGIN = 20
NB = 16
NSETS = 8
TILES = 8
WIDTH = 4096
NY = 4
NZ = 8
CAP = 2
PER_ROW = NZ * CAP
CHUNK = 16
PARTS = TR // CHUNK
NC = 2 * PARTS
HALO = 24
XROWS = 128
WIN = 384
OUTW = 256
NWIN = WIDTH // OUTW
XBLOCKS = 34
HALVES = 2
HWIN = NWIN // HALVES
QWIN = HWIN // 2
LAG = 2


PLACE, STARTS, PICK, WHICH = KP, 2 * KP, 3 * KP, 4 * KP
VARIANTS = (5, 6, 8)


def plan_kernel(inter, offset, basis_row, basis_col, table, brow, bcol):
    me = lax.axis_index("visit")
    my_y, my_z = me // NZ, lax.rem(me, NZ)
    owner = inter[...]
    column = lax.rem(owner, NZ)
    lane = lax.broadcasted_iota(jnp.int32, (KP, KP), 1)
    visit_z = lax.rem(lax.broadcasted_iota(jnp.int32, (KP, KP), 0), NZ)
    rank = jnp.zeros((KP, KP), jnp.int32)
    place = jnp.zeros((KP, KP), jnp.int32)
    for k in range(KP - 1):
        later = lane > k
        rank += ((owner == owner[:, k : k + 1]) & later).astype(jnp.int32)
        place += ((column == column[:, k : k + 1]) & later).astype(jnp.int32)
    slot = lax.rem(my_y + NY - owner // NZ, NY) * PER_ROW + visit_z * CAP + rank
    starts = jnp.zeros((KP, KP), jnp.int32)
    for j in range(CAP):
        found = jnp.sum(jnp.where((owner == me) & (rank == j), offset[...], 0), axis=1, keepdims=True)
        starts = jnp.where(lane == j, found, starts)
    pick = jnp.zeros((KP, KP), jnp.int32)
    for p in range(NZ):
        found = jnp.sum(jnp.where((column == my_z) & (place == p), slot, 0), axis=1, keepdims=True)
        pick = jnp.where(lane == p, found, pick)
    most = jnp.max(place) + 1
    which = jnp.zeros((8, KP), jnp.int32)
    for n in VARIANTS[:-1]:
        which += (most > n).astype(jnp.int32)
    table[0:PLACE] = lax.rem(visit_z - column + NZ, NZ)
    table[PLACE:STARTS] = place
    table[STARTS:PICK] = starts
    table[PICK:WHICH] = pick
    table[WHICH:] = which

    def spread(values, width, at):
        tap = lax.broadcasted_iota(jnp.int32, (KW, width), 0)
        hot = lax.broadcasted_iota(jnp.int32, (KW, width), 1) == at(tap)
        return jnp.dot(
            values, hot.astype(F32), precision=lax.Precision.HIGHEST, preferred_element_type=F32
        )

    brow[...] = spread(basis_row[...], PIECE, lambda tap: tap + HALO - MARGIN)
    bcol[...] = spread(basis_col[...], OUTW, lambda tap: lax.rem(OUTW - tap, OUTW))


def plan(inter, offset, basis_row, basis_col):
    return pl.pallas_call(
        plan_kernel,
        out_shape=(
            jax.ShapeDtypeStruct((WHICH + 8, KP), jnp.int32),
            jax.ShapeDtypeStruct((NB, PIECE), F32),
            jax.ShapeDtypeStruct((NB, OUTW), F32),
        ),
        in_specs=[pl.BlockSpec(memory_space=pltpu.VMEM)] * 4,
        out_specs=(pl.BlockSpec(memory_space=pltpu.VMEM),) * 3,
        name="plan",
    )(inter, offset, basis_row, basis_col)


def split(x):
    high = x.astype(BF16)
    return high, (x - high.astype(F32)).astype(BF16)


def main_kernel(slots, *refs):
    table, tile_coef, coefs, flux_in, var_in, brow, bcol, conv, var_out = refs[:9]
    yr, zs, zr = (refs[9 + n * NC : 9 + (n + 1) * NC] for n in range(3))
    ys, flux_strip, var_strip, blocks, power = refs[9 + 3 * NC : 14 + 3 * NC]
    x_full, x_split, row_band, cb_high, cb_low, rw_high, rw_low = refs[14 + 3 * NC : 21 + 3 * NC]
    in_sem, own_sem, ys_sem, yr_sem, zs_sem, zr_sem, hs_sem, hr_sem = refs[21 + 3 * NC :]
    strips = (flux_strip, var_strip)

    me = lax.axis_index("visit")
    tile = lax.axis_index("tile")
    y, z = me // NZ, lax.rem(me, NZ)

    def y_peer(r):
        return (lax.rem(y + r, NY) * NZ + z, tile)

    def z_peer(d):
        return (y * NZ + lax.rem(z + d, NZ), tile)

    def t_peer(s):
        return (me, lax.rem(tile + s + TILES, TILES))

    inputs = [
        pltpu.make_async_copy(source, target, in_sem.at[n])
        for n, (source, target) in enumerate(zip((flux_in, var_in), strips))
    ]
    for copy in inputs:
        copy.start()
    barrier = pltpu.get_barrier_semaphore()
    peers = [y_peer(r) for r in range(1, NY)] + [z_peer(d) for d in range(1, NZ)] + [t_peer(1), t_peer(-1)]
    for peer in peers:
        pl.semaphore_signal(barrier, inc=1, device_id=peer, device_id_type=MESH)
    pl.semaphore_wait(barrier, len(peers))

    def y_copy(c, r):
        return pltpu.make_async_remote_copy(
            src_ref=ys.at[pl.ds((c * NY + r) * PER_ROW, PER_ROW)],
            dst_ref=yr[c].at[pl.ds(r * PER_ROW, PER_ROW)],
            send_sem=ys_sem.at[c, r - 1],
            recv_sem=yr_sem.at[c, r - 1],
            device_id=y_peer(r),
            device_id_type=MESH,
        )

    def own_copy(c):
        return pltpu.make_async_copy(
            ys.at[pl.ds(c * NY * PER_ROW, PER_ROW)], yr[c].at[pl.ds(0, PER_ROW)], own_sem.at[c]
        )

    def z_copy(c, d):
        return pltpu.make_async_remote_copy(
            src_ref=zs[c].at[pl.ds(d * slots, slots)],
            dst_ref=zr[c].at[pl.ds(d * slots, slots)],
            send_sem=zs_sem.at[c, d - 1],
            recv_sem=zr_sem.at[c, d - 1],
            device_id=z_peer(d),
            device_id_type=MESH,
        )

    def halo_copy(which):
        source, target, step = ((TR, 0, 1), (HALO, HALO + TR, -1))[which]
        return pltpu.make_async_remote_copy(
            src_ref=x_full.at[pl.ds(source, HALO)],
            dst_ref=x_full.at[pl.ds(target, HALO)],
            send_sem=hs_sem.at[which],
            recv_sem=hr_sem.at[which],
            device_id=t_peer(step),
            device_id_type=MESH,
        )

    lane = lax.broadcasted_iota(jnp.int32, (CHUNK, PIECE), 1)

    def take_in(plane):
        inputs[plane].wait()

        def one(k, _):
            at = pl.ds(pl.multiple_of(k * PIECE, PIECE), PIECE)
            blocks[plane * KP + k] = strips[plane][:, at]
            return 0

        lax.fori_loop(0, KP, one, 0)

    def cut(c):
        first = c // PARTS * KP
        rows = pl.ds(pl.multiple_of(lax.rem(c, PARTS) * CHUNK, CHUNK), CHUNK)

        def one(e, _):
            r = lax.rem(e + 1, NY)
            visits = STARTS + lax.rem(y + r, NY) * NZ
            pieces, shifts = [], []
            for vz in range(NZ):
                for j in range(CAP):
                    start = table[visits + vz, j]
                    block = start // PIECE
                    shift = jnp.full((CHUNK, PIECE), start - block * PIECE, jnp.int32)
                    here = blocks[first + block, rows, :]
                    beside = blocks[first + jnp.minimum(block + 1, KP - 1), rows, :]
                    pieces.append(jnp.where(lane >= shift, here, beside))
                    shifts.append(shift)
            for bit in range(7):
                turned = [pltpu.roll(piece, PIECE - (1 << bit), 1) for piece in pieces]
                pieces = [
                    jnp.where((shift & (1 << bit)) != 0, after, piece)
                    for shift, after, piece in zip(shifts, turned, pieces)
                ]
            for slot, piece in enumerate(pieces):
                ys[(c * NY + r) * PER_ROW + slot] = piece
            for chunk in range(NC):

                @pl.when((c == chunk) & (e < NY - 1))
                def _():
                    y_copy(chunk, r).start()

            return 0

        lax.fori_loop(0, NY, one, 0)

    def y_start(c):
        own_copy(c).start()

    def forward(c):
        own_copy(c).wait()
        for r in range(1, NY):
            y_copy(c, r).wait_recv()

        def one(e, _):
            half = (e + 1) // 2
            d = NZ // 2 + jnp.where(lax.rem(e, 2) == 1, -half, half)
            row = PICK + y * NZ + lax.rem(z + d, NZ)
            for p in range(slots):
                zs[c][d * slots + p] = yr[c][table[row, p]]
            z_copy(c, d).start()
            return 0

        lax.fori_loop(0, NZ - 1, one, 0)
        for p in range(slots):
            zr[c][p] = yr[c][table[PICK + me, p]]

    def assemble(c, out, row, scale=None):
        for d in range(1, NZ):
            z_copy(c, d).wait_recv()

        def one(k, _):
            piece = zr[c][table[me, k] * slots + table[PLACE + me, k]]
            at = pl.ds(pl.multiple_of(k * PIECE, PIECE), PIECE)
            out[pl.ds(row, CHUNK), at] = piece if scale is None else piece * scale
            return 0

        lax.fori_loop(0, KP, one, 0)

    chosen = tile_coef[me, tile]

    def bands():
        rows = [coefs[chosen, b] * brow[b : b + 1, :] for b in range(NB)]
        for b in range(NB):
            band = pltpu.roll(jnp.broadcast_to(rows[b], (TR, PIECE)), 0, 1, stride=1, stride_axis=0)
            high, low = split(band)
            row_band[b * TR : (b + 1) * TR, 0:PIECE] = high
            row_band[b * TR : (b + 1) * TR, PIECE : 2 * PIECE] = low
            row_band[b * TR : (b + 1) * TR, 2 * PIECE : 3 * PIECE] = high
        whole = lax.dot_general(
            jnp.concatenate(rows, axis=0),
            bcol[...],
            (((0,), (0,)), ((), ())),
            precision=lax.Precision.HIGHEST,
            preferred_element_type=F32,
        )
        def one(b, _):
            line = bcol[pl.ds(b, 1), :]
            for part in range(WIN // 128):
                turned = pltpu.roll(
                    jnp.broadcast_to(line, (128, OUTW)), (part * 128) % OUTW, 1, stride=1, stride_axis=0
                )
                tap = (
                    lax.broadcasted_iota(jnp.int32, (128, OUTW), 0)
                    + part * 128
                    - lax.broadcasted_iota(jnp.int32, (128, OUTW), 1)
                )
                high, low = split(jnp.where((tap >= 0) & (tap < KW), turned, 0.0))
                place = pl.ds(pl.multiple_of(b * WIN + part * 128, 128), 128)
                cb_high[place, :] = high
                cb_low[place, :] = low
            return 0

        lax.fori_loop(0, NB, one, 0)
        power[0] = jnp.sum(whole * whole)

    def expand():
        row = lax.broadcasted_iota(jnp.int32, (XROWS, PIECE), 0)
        lane = lax.broadcasted_iota(jnp.int32, (XROWS, PIECE), 1)
        first = jnp.where(tile == 0, HALO, 0)
        last = jnp.where(tile == TILES - 1, HALO + TR, HALO + TR + HALO)
        rows_in = (row >= first) & (row < last)

        def one(j, _):
            here = pl.multiple_of(jnp.minimum(j, KP - 1) * PIECE, PIECE)
            before = pl.multiple_of(jnp.minimum(jnp.maximum(j - 1, 0), KP - 1) * PIECE, PIECE)
            both = jnp.where(
                lane < MARGIN,
                pltpu.roll(x_full[:, pl.ds(before, PIECE)], MARGIN, 1),
                pltpu.roll(x_full[:, pl.ds(here, PIECE)], MARGIN, 1),
            )
            column = j * PIECE + lane - MARGIN
            high, low = split(jnp.where(rows_in & (column >= 0) & (column < WIDTH), both, 0.0))
            place = pl.ds(pl.multiple_of(j * PIECE, PIECE), PIECE)
            x_split[0:XROWS, place] = high
            x_split[XROWS : 2 * XROWS, place] = high
            x_split[2 * XROWS : 3 * XROWS, place] = low
            return 0

        lax.fori_loop(0, XBLOCKS, one, 0)

    def convolve(h, _):
        def rows(m, _):
            high, low = split(
                jnp.dot(
                    row_band[...],
                    x_split[:, pl.ds(pl.multiple_of((h * HWIN + m) * OUTW, OUTW), OUTW)],
                    preferred_element_type=F32,
                )
            )
            now = pl.ds(pl.multiple_of((m + 1) * TR, TR), TR)
            before = pl.ds(pl.multiple_of(m * TR, TR), TR)
            for out, value in ((rw_high, high), (rw_low, low)):
                for b in range(NB):
                    part = value[b * TR : (b + 1) * TR]
                    out[now, b * WIN : b * WIN + OUTW] = part
                    out[before, b * WIN + OUTW : (b + 1) * WIN] = part[:, 0 : WIN - OUTW]
            return 0

        def cols(q, _):
            at = pl.ds(pl.multiple_of(TR + q * QWIN * TR, TR), QWIN * TR)
            total = jnp.dot(rw_high[at, :], cb_high[...], preferred_element_type=F32)
            total += jnp.dot(rw_high[at, :], cb_low[...], preferred_element_type=F32)
            total += jnp.dot(rw_low[at, :], cb_high[...], preferred_element_type=F32)
            for n in range(QWIN):
                first = pl.multiple_of((h * HWIN + q * QWIN + n) * OUTW, OUTW)
                conv[:, pl.ds(first, OUTW)] = total[n * TR : (n + 1) * TR, :]
            return 0

        lax.fori_loop(0, HWIN + 1, rows, 0)
        lax.fori_loop(0, HWIN // QWIN, cols, 0)
        return 0

    def step(i, _):
        @pl.when(i < NC)
        def _():
            cut(i)

        for c in range(NC):

            @pl.when(i == c)
            def _():
                y_start(c)

        @pl.when(i == PARTS - 1)
        def _():
            take_in(1)

        for c in range(NC):

            @pl.when(i == c + LAG)
            def _():
                forward(c)

        @pl.when(i == PARTS - 1 + LAG)
        def _():
            bands()

        @pl.when(i == NC - 3 + LAG)
        def _():
            for part in range(PARTS):
                assemble(part, x_full, HALO + part * CHUNK)
            halo_copy(0).start()
            halo_copy(1).start()

        return 0

    take_in(0)
    lax.fori_loop(0, NC + LAG, step, 0)
    halo_copy(0).wait_recv()
    halo_copy(1).wait_recv()
    expand()
    lax.fori_loop(0, HALVES, convolve, 0)
    for part in range(PARTS):
        assemble(PARTS + part, var_out, part * CHUNK, power[0])
    halo_copy(0).wait_send()
    halo_copy(1).wait_send()
    for c in range(NC):
        for r in range(1, NY):
            y_copy(c, r).wait_send()
        for d in range(1, NZ):
            z_copy(c, d).wait_send()


def exchange(slots, table, tile_coef, coefs, flux, var, brow, bcol):
    smem = pl.BlockSpec(memory_space=pltpu.SMEM)
    vmem = pl.BlockSpec(memory_space=pltpu.VMEM)
    hbm = pl.BlockSpec(memory_space=pl.ANY)
    scratch = [pltpu.VMEM((NY * PER_ROW, CHUNK, PIECE), F32)] * NC
    scratch += [pltpu.VMEM((NZ * slots, CHUNK, PIECE), F32)] * (2 * NC)
    scratch += [
        pltpu.VMEM((NC * NY * PER_ROW, CHUNK, PIECE), F32),
        pltpu.VMEM((TR, WIDTH), F32),
        pltpu.VMEM((TR, WIDTH), F32),
        pltpu.VMEM((2 * KP, TR, PIECE), F32),
        pltpu.SMEM((1,), F32),
        pltpu.VMEM((XROWS, WIDTH), F32),
        pltpu.VMEM((3 * XROWS, XBLOCKS * PIECE), BF16),
        pltpu.VMEM((NB * TR, 3 * PIECE), BF16),
        pltpu.VMEM((NB * WIN, OUTW), BF16),
        pltpu.VMEM((NB * WIN, OUTW), BF16),
        pltpu.VMEM(((HWIN + 2) * TR, NB * WIN), BF16),
        pltpu.VMEM(((HWIN + 2) * TR, NB * WIN), BF16),
        pltpu.SemaphoreType.DMA((2,)),
        pltpu.SemaphoreType.DMA((NC,)),
        pltpu.SemaphoreType.DMA((NC, NY - 1)),
        pltpu.SemaphoreType.DMA((NC, NY - 1)),
        pltpu.SemaphoreType.DMA((NC, NZ - 1)),
        pltpu.SemaphoreType.DMA((NC, NZ - 1)),
        pltpu.SemaphoreType.DMA((2,)),
        pltpu.SemaphoreType.DMA((2,)),
    ]
    return pl.pallas_call(
        functools.partial(main_kernel, slots),
        out_shape=(
            jax.ShapeDtypeStruct((TR, WIDTH), F32),
            jax.ShapeDtypeStruct((TR, WIDTH), F32),
        ),
        in_specs=[smem] * 3 + [hbm] * 2 + [vmem] * 2,
        out_specs=(vmem, vmem),
        scratch_shapes=scratch,
        compiler_params=pltpu.CompilerParams(
            collective_id=slots, has_side_effects=True, vmem_limit_bytes=60 << 20
        ),
        cost_estimate=pl.CostEstimate(flops=10**10, bytes_accessed=6 << 20, transcendentals=0),
        name=f"exchange_{slots}",
    )(table, tile_coef, coefs, flux, var, brow, bcol)


def local(
    science,
    science_var,
    template,
    template_var,
    intersection,
    col_offset,
    basis_row,
    basis_col,
    coef_sets,
    tile_coef,
):
    table, brow, bcol = plan(intersection[:, :, 0], col_offset, basis_row, basis_col)
    convolved, variance = lax.switch(
        table[WHICH, 0],
        [functools.partial(exchange, n) for n in VARIANTS],
        table,
        tile_coef,
        coef_sets,
        template[0],
        template_var[0],
        brow,
        bcol,
    )
    return science - convolved[None], science_var + variance[None]


def solution(mesh):
    split3 = P("visit", "tile", None)
    return jax.shard_map(
        local,
        mesh=mesh,
        in_specs=(split3, split3, split3, split3, P(), P(), P(), P(), P(), P()),
        out_specs=(split3, split3),
        check_vma=False,
    )
```
